32 devices in a mesh: groups: 2 (over y), inst: 4 (over z), tp: 4 (over x, core).
Axes of the slice: x: 2, y: 2, z: 4, core: 2. Of those that a mesh axis runs over, the one named last changes fastest.
Arguments:
- hidden: bfloat16 [192, 32, 5120], P(('groups', 'inst'), None, 'tp'), parts along dimension 0, may hold values from -400 to 400
- norm_gain: float32 [5120], replicated, may hold values from 0.1 to 1.9
- w_query: bfloat16 [5120, 4096], P('inst', 'tp'), may hold values from -0.078125 to 0.078125
- w_key: bfloat16 [5120, 512], P('inst', 'tp'), may hold values from -0.078125 to 0.078125
- w_value: bfloat16 [5120, 512], P('inst', 'tp'), may hold values from -0.078125 to 0.078125
- bias_query: float32 [4096], P('tp'), may hold values from -3 to 3
- bias_key: float32 [512], P('tp'), may hold values from -81 to 81
- bias_value: float32 [512], P('tp'), may hold values from -3 to 3
- prefix_blocks: int32 [8], P(('groups', 'inst')), parts along dimension 0, may hold values from 1 to 24, as said below
- block_target: int32 [8, 24], P(('groups', 'inst')), parts along dimension 0, may hold values from -1 to 47, as said below
- cache_slot: int32 [8, 24], P(('groups', 'inst')), parts along dimension 0, may hold values from 0 to 23, each once within a row
Outputs:
- attn_out: bfloat16 [96, 32, 4096], P(('groups', 'inst'), None, 'tp'), parts along dimension 0
- key_cache: bfloat16 [192, 32, 512], P(('groups', 'inst'), None, 'tp'), parts along dimension 0
- value_cache: bfloat16 [192, 32, 512], P(('groups', 'inst'), None, 'tp'), parts along dimension 0
The draws below stay inside these ranges and needn't reach their ends.
There are 2 independent parts, one for each index of `groups`. The reference program is written for one: setup_inputs(seed, part) draws one part's arguments, and reference() takes and returns one part's arrays. A program takes and returns all parts, laid end to end along the dimension named above; an argument that names none is the same for every part. Nothing has to cross between parts.
Inputs may be any that keep to these rules, and one draw needn't show every extreme that they name: `prefix_blocks`: some instance holds 24 blocks; all prefixes together hold exactly 48 blocks. `block_target`: for a live slot, b * 12 + c names slot c of balancing instance b; dead slots hold -1. Every balancing slot is named exactly once. No instance sends more than 6 blocks to one balancing instance, and in every draw some instance sends exactly 6 to some balancing instance.
All inputs are finite; a program needn't handle non-finite values.
Results may differ from the reference program's by a relative error of at most 0.0018.
The reference program's roundings to bfloat16 on the way count: a program that leaves them out, or rounds other values in their place, can miss the bound.
Values may be sent and summed in bfloat16 or wider, within the bound.
A program may use at most 128 MiB of HBM per device.

```python
import math
import jax
import jax.numpy as jnp
from jax import lax

D = 5120
H = 32
KVH = 4
HD = 128
BLOCK = 32
OWN = 24
BAL = 12
N_INST = 4


def layout(key):
    units = OWN - 1
    total_units = N_INST * units
    full_owner = jax.random.randint(jax.random.fold_in(key, 101), (), 0, N_INST)
    order = jax.random.permutation(jax.random.fold_in(key, 102), total_units).astype(jnp.int32)
    owner_of_unit = jnp.arange(total_units, dtype=jnp.int32) // units
    score = jnp.where(owner_of_unit == full_owner, order - total_units, order)
    ranking = jnp.argsort(jnp.argsort(score))
    chosen = (ranking < N_INST * (BAL - 1)).astype(jnp.int32)
    counts = 1 + jnp.sum(chosen.reshape(N_INST, units), axis=1)
    start = jnp.cumsum(counts) - counts
    slots = jnp.arange(OWN, dtype=jnp.int32)
    index = start[:, None] + slots[None, :]
    live = slots[None, :] < counts[:, None]
    offset = jax.random.randint(jax.random.fold_in(key, 103), (), 0, N_INST)
    relabel = jax.random.permutation(jax.random.fold_in(key, 104), N_INST).astype(jnp.int32)
    rotation = jax.random.randint(jax.random.fold_in(key, 105), (N_INST,), 0, BAL)
    balancer = relabel[(index + offset) % N_INST]
    place = (index // N_INST + rotation[balancer]) % BAL
    target = jnp.where(live, balancer * BAL + place, -1)
    return (counts.astype(jnp.int32), target.astype(jnp.int32))


def draw_prefix_blocks(key, part):
    shared = layout(key)
    return shared[0]


def draw_block_target(key, part):
    shared = layout(key)
    return shared[1]


def draw_hidden(key, part):
    key = jax.random.fold_in(key, 7)
    first_key, second_key, third_key = jax.random.split(key, 3)
    base = jnp.clip(jax.random.normal(first_key, (N_INST * OWN, BLOCK, D), jnp.float32), -4.0, 4.0)
    row_scale = jnp.exp(jax.random.uniform(second_key, (N_INST * OWN, BLOCK, 1), jnp.float32, 0.0, math.log(10.0)))
    col_scale = jnp.exp(jax.random.uniform(third_key, (1, 1, D), jnp.float32, 0.0, math.log(10.0)))
    values = base * row_scale * col_scale
    return values.astype(jnp.bfloat16)


def draw_bias_key(key, part):
    key = jax.random.fold_in(key, 9)
    first_key = jax.random.fold_in(key, 0)
    values = 0.5 * jnp.clip(jax.random.normal(first_key, (KVH * HD,), jnp.float32), -4.0, 4.0)
    return values.astype(jnp.float32)


def shard_levels(stream_key, shape, cuts, least, high):
    gain, own = 1.0, jax.random.fold_in(stream_key, 6)
    for position, shards_of in cuts:
        steps = jnp.exp(jax.random.uniform(jax.random.fold_in(own, position), (shards_of,), jnp.float32, least / len(cuts), high / len(cuts)))
        gain = gain * jnp.repeat(steps, shape[position] // shards_of).reshape([-1 if axis == position else 1 for axis in range(len(shape))])
    return gain


def noise(key, extent, deviation, limit, cuts=(), kind=jnp.bfloat16):
    result = deviation * jax.random.normal(key, extent, jnp.float32)
    if cuts:
        result = result * shard_levels(key, extent, cuts, -0.22, 0.18)
    return jnp.clip(result, -limit, limit).astype(kind)


def setup_inputs(seed: int = 0, part: int = 0) -> dict:
    streams_of = jax.random.split(jax.random.key(seed), 12)
    own_keys = jax.random.split(jax.random.fold_in(streams_of[11], part), 12)
    hidden = draw_hidden(jax.random.fold_in(jax.random.fold_in(streams_of[11], part), 71), part)
    norm_gain = jnp.clip(1.0 + 0.18 * jax.random.normal(streams_of[1], (D,), jnp.float32), 0.1, 1.9)
    w_query = noise(streams_of[2], (D, H * HD), D ** -0.5, 0.078125, ((0, 4), (1, 4)))
    w_key = noise(streams_of[3], (D, KVH * HD), D ** -0.5, 0.078125, ((0, 4), (1, 4)))
    w_value = noise(streams_of[4], (D, KVH * HD), D ** -0.5, 0.078125, ((0, 4), (1, 4)))
    bias_query = noise(streams_of[5], (H * HD,), 0.5, 3.0, ((0, 4),), jnp.float32)
    bias_key = draw_bias_key(jax.random.fold_in(streams_of[11], 71), part)
    bias_value = noise(streams_of[7], (KVH * HD,), 0.5, 3.0, ((0, 4),), jnp.float32)
    prefix_blocks = draw_prefix_blocks(jax.random.fold_in(jax.random.fold_in(streams_of[11], part), 71), part)
    block_target = draw_block_target(jax.random.fold_in(jax.random.fold_in(streams_of[11], part), 71), part)
    cache_slot = jax.vmap(lambda own: jax.random.permutation(own, OWN))(jax.random.split(own_keys[10], N_INST)).reshape((N_INST, OWN)).astype(jnp.int32)
    return {"hidden": hidden, "norm_gain": norm_gain, "w_query": w_query, "w_key": w_key, "w_value": w_value, "bias_query": bias_query, "bias_key": bias_key, "bias_value": bias_value, "prefix_blocks": prefix_blocks, "block_target": block_target, "cache_slot": cache_slot}


ROPE_BASE = 1000000.0
NORM_EPS = 1e-06

def rotate(values, positions):
    width = values.shape[-1]
    half = width // 2
    freqs = ROPE_BASE ** (-(jnp.arange(half, dtype=jnp.float32) * 2.0 / width))
    angles = positions.astype(jnp.float32)[:, None] * freqs[None, :]
    cosine = jnp.cos(angles)[:, None, :]
    sine = jnp.sin(angles)[:, None, :]
    first = values[..., :half]
    second = values[..., half:]
    return jnp.concatenate([first * cosine - second * sine, second * cosine + first * sine], axis=-1)

def reference(hidden, norm_gain, w_query, w_key, w_value, bias_query, bias_key, bias_value, prefix_blocks, block_target, cache_slot):
    group = H // KVH
    total_rows = OWN * BLOCK
    positions = jnp.arange(total_rows, dtype=jnp.int32)
    causal = positions[:, None] >= positions[None, :]
    scale_factor = 1.0 / math.sqrt(HD)

    def owner(pack):
        rows, count, perm = pack
        values = rows.reshape(total_rows, D).astype(jnp.float32)
        inverse_rms = lax.rsqrt(lax.optimization_barrier(jnp.mean(values * values, axis=-1, keepdims=True)) + NORM_EPS)
        normed = (values * inverse_rms * norm_gain.astype(jnp.float32)).astype(jnp.bfloat16)
        query = jnp.dot(normed, w_query, preferred_element_type=jnp.float32) + bias_query.astype(jnp.float32)
        query = rotate(query.reshape(total_rows, H, HD), positions).reshape(total_rows, H * HD).astype(jnp.bfloat16)
        keys = jnp.dot(normed, w_key, preferred_element_type=jnp.float32) + bias_key.astype(jnp.float32)
        keys = rotate(keys.reshape(total_rows, KVH, HD), positions).reshape(total_rows, KVH * HD).astype(jnp.bfloat16)
        vals = (jnp.dot(normed, w_value, preferred_element_type=jnp.float32) + bias_value.astype(jnp.float32)).astype(jnp.bfloat16)
        query_heads = query.astype(jnp.float32).reshape(total_rows, KVH, group, HD)
        key_heads = keys.astype(jnp.float32).reshape(total_rows, KVH, HD)
        value_heads = vals.astype(jnp.float32).reshape(total_rows, KVH, HD)

        def head(query_group):
            scores = jnp.einsum('rkd,skd->krs', query_group, key_heads) * scale_factor
            scores = jnp.where(causal[None], scores, -jnp.inf)
            largest = lax.optimization_barrier(jnp.max(scores, axis=-1, keepdims=True))
            expo = jnp.exp(scores - largest)
            probs = (expo / lax.optimization_barrier(jnp.sum(expo, axis=-1, keepdims=True))).astype(jnp.bfloat16)
            mixed = jnp.einsum('krs,skd->rkd', probs.astype(jnp.float32), value_heads)
            return mixed.astype(jnp.bfloat16)
        heads_out = lax.map(head, jnp.moveaxis(query_heads, 2, 0))
        attention = jnp.transpose(heads_out, (1, 2, 0, 3)).reshape(OWN, BLOCK, H * HD)
        live = (jnp.arange(OWN, dtype=jnp.int32) < count)[:, None, None]
        key_blocks = jnp.where(live, keys.reshape(OWN, BLOCK, KVH * HD), jnp.zeros((), jnp.bfloat16))
        value_blocks = jnp.where(live, vals.reshape(OWN, BLOCK, KVH * HD), jnp.zeros((), jnp.bfloat16))
        key_out = jnp.zeros((OWN, BLOCK, KVH * HD), jnp.bfloat16).at[perm].set(key_blocks)
        value_out = jnp.zeros((OWN, BLOCK, KVH * HD), jnp.bfloat16).at[perm].set(value_blocks)
        return (attention, key_out, value_out)
    attention, key_out, value_out = lax.map(owner, (hidden.reshape(N_INST, OWN, BLOCK, D), prefix_blocks, cache_slot))
    attention = attention.reshape(N_INST * OWN, BLOCK, H * HD)
    flat_target = block_target.reshape(-1)
    index = jnp.where(flat_target >= 0, flat_target, N_INST * BAL).astype(jnp.int32)
    attn_out = jnp.zeros((N_INST * BAL, BLOCK, H * HD), jnp.bfloat16).at[index].set(attention, mode='drop')
    return (attn_out, key_out.reshape(N_INST * OWN, BLOCK, KVH * HD), value_out.reshape(N_INST * OWN, BLOCK, KVH * HD))
```

```python
import functools
import math

import jax
import jax.numpy as jnp
from jax import lax
from jax.experimental import pallas as pl
from jax.experimental.pallas import tpu as pltpu
from jax.sharding import PartitionSpec as P

HD = 128
BAL = 12


ROPE_BASE = 1000000.0
NORM_EPS = 1e-06


def rotate(values, positions):
    width = values.shape[-1]
    half = width // 2
    freqs = ROPE_BASE ** (-(jnp.arange(half, dtype=jnp.float32) * 2.0 / width))
    angles = positions.astype(jnp.float32)[:, None] * freqs[None, :]
    cosine = jnp.cos(angles)[:, None, :]
    sine = jnp.sin(angles)[:, None, :]
    first = values[..., :half]
    second = values[..., half:]
    return jnp.concatenate(
        [first * cosine - second * sine, second * cosine + first * sine], axis=-1
    )


def project(whole, positions, norm_gain, w_query, w_key, w_value, bias_query, bias_key, bias_value):
    values = whole.astype(jnp.float32)
    inverse_rms = lax.rsqrt(jnp.mean(values * values, axis=-1, keepdims=True) + NORM_EPS)
    normed = (values * inverse_rms * norm_gain).astype(jnp.bfloat16)
    total_rows = normed.shape[0]
    query_sum = jnp.dot(
        normed,
        lax.all_gather(w_query, "inst", axis=0, tiled=True),
        preferred_element_type=jnp.float32,
    )
    key_sum = jnp.dot(
        normed,
        lax.all_gather(w_key, "inst", axis=0, tiled=True),
        preferred_element_type=jnp.float32,
    )
    value_sum = jnp.dot(
        normed,
        lax.all_gather(w_value, "inst", axis=0, tiled=True),
        preferred_element_type=jnp.float32,
    )
    query = query_sum
    keys = key_sum
    vals = value_sum
    query = rotate((query + bias_query).reshape(total_rows, -1, HD), positions)
    query = query.reshape(total_rows, -1).astype(jnp.bfloat16)
    keys = rotate((keys + bias_key).reshape(total_rows, -1, HD), positions)
    keys = keys.reshape(total_rows, -1).astype(jnp.bfloat16)
    vals = (vals + bias_value).astype(jnp.bfloat16)
    return (query, keys, vals)


def pick_slots(labels_place, labels_live, count):
    items = jnp.arange(labels_place.shape[0], dtype=jnp.int32)
    wanted = (labels_place[None, :] == jnp.arange(count, dtype=jnp.int32)[:, None]) & (
        labels_live[None, :] == 1
    )
    return jnp.sum(jnp.where(wanted, items[None, :], 0), axis=1)


def shards(
    hidden,
    norm_gain,
    w_query,
    w_key,
    w_value,
    bias_query,
    bias_key,
    bias_value,
    prefix_blocks,
    block_target,
    cache_slot,
):
    owned, width_block, part_width = hidden.shape
    peers = lax.axis_size("inst")
    pair = -(-owned // peers)
    total_rows = owned * width_block
    slots = jnp.arange(owned, dtype=jnp.int32)
    live = slots < prefix_blocks[0]
    target = block_target[0]
    dest = jnp.where(live, target // BAL, -1)
    place = jnp.where(live, target % BAL, 0)
    earlier = (dest[:, None] == dest[None, :]) & live[None, :] & (slots[None, :] < slots[:, None])
    rank = jnp.sum(earlier.astype(jnp.int32), axis=1)
    item_of_slot = jnp.where(live, dest * pair + rank, -1)
    items = jnp.arange(peers * pair, dtype=jnp.int32)
    matched = item_of_slot[None, :] == items[:, None]
    present = jnp.any(matched, axis=1)
    source = jnp.sum(jnp.where(matched, slots[None, :], 0), axis=1)
    own_positions = jnp.arange(total_rows, dtype=jnp.int32)
    zero_half = jnp.zeros((), jnp.bfloat16)
    whole = lax.all_gather(hidden.reshape(total_rows, part_width), "tp", axis=1, tiled=True)
    query, keys, vals = project(
        whole, own_positions, norm_gain, w_query, w_key, w_value, bias_query, bias_key, bias_value
    )
    kv_here = keys.shape[1] // HD
    group = query.shape[1] // (HD * kv_here)
    query_heads = query.reshape(total_rows, kv_here, group, HD)
    key_heads = keys.reshape(total_rows, kv_here, HD)
    value_heads = vals.reshape(total_rows, kv_here, HD)
    causal = own_positions[:, None] >= own_positions[None, :]
    scale_factor = 1.0 / math.sqrt(HD)

    def head(query_group):
        scores = (
            jnp.einsum("rkd,skd->krs", query_group, key_heads, preferred_element_type=jnp.float32)
            * scale_factor
        )
        scores = jnp.where(causal[None], scores, -jnp.inf)
        largest = jnp.max(scores, axis=-1, keepdims=True)
        expo = jnp.exp(scores - largest)
        probs = (expo / jnp.sum(expo, axis=-1, keepdims=True)).astype(jnp.bfloat16)
        mixed = jnp.einsum("krs,skd->rkd", probs, value_heads, preferred_element_type=jnp.float32)
        return mixed.astype(jnp.bfloat16)

    heads_out = lax.map(head, jnp.moveaxis(query_heads, 2, 0))
    attention = jnp.transpose(heads_out, (1, 2, 0, 3)).reshape(owned, width_block, -1)
    perm = cache_slot[0]
    inverse = jnp.sum(jnp.where(perm[None, :] == slots[:, None], slots[None, :], 0), axis=1)
    live_blocks = live[:, None, None]
    key_blocks = jnp.where(live_blocks, keys.reshape(owned, width_block, -1), zero_half)
    value_blocks = jnp.where(live_blocks, vals.reshape(owned, width_block, -1), zero_half)
    key_cache = jnp.take(key_blocks, inverse, axis=0)
    value_cache = jnp.take(value_blocks, inverse, axis=0)
    send_out = jnp.where(present[:, None, None], jnp.take(attention, source, axis=0), zero_half)
    send_out = send_out.reshape(peers, pair, width_block, -1)
    out_labels = jnp.stack([jnp.take(place, source), present.astype(jnp.int32)], axis=-1).reshape(
        peers, pair, 2
    )
    got_out, got_out_labels = (
        lax.all_to_all(send_out, "inst", split_axis=0, concat_axis=0, tiled=True),
        lax.all_to_all(out_labels, "inst", split_axis=0, concat_axis=0, tiled=True),
    )
    got_out = got_out.reshape(peers * pair, width_block, -1)
    got_out_labels = got_out_labels.reshape(peers * pair, 2)
    chosen_out = pick_slots(got_out_labels[:, 0], got_out_labels[:, 1], BAL)
    attn_out = jnp.take(got_out, chosen_out, axis=0)
    return (attn_out, key_cache, value_cache)


TILE = 256
PIECE = 256
MESH = pl.DeviceIdType.MESH


def fused_kernel(
    n,
    tp,
    pair,
    source_ref,
    hid_ref,
    wq_ref,
    wk_ref,
    wv_ref,
    gain_ref,
    bias_ref,
    cos_ref,
    sin_ref,
    lab_ref,
    key_ref,
    val_ref,
    got_ref,
    lab_out,
    hbuf,
    normed,
    wfull,
    qbuf,
    atb,
    sendbuf,
    loc_sem,
    h_send,
    h_recv,
    z_send,
    z_recv,
    y_send,
    y_recv,
    d_send,
    d_recv,
    l_send,
    l_recv,
):
    g = lax.axis_index("groups")
    i = lax.axis_index("inst")
    t = lax.axis_index("tp")
    x, core = t // 2, t % 2
    t_core = 2 * x + (1 - core)
    t_far = 2 * (1 - x) + core
    t_diag = 2 * (1 - x) + (1 - core)
    tokens, part = hid_ref.shape
    rows = wq_ref.shape[0]
    half = rows // 2
    pieces = wfull.shape[0]
    peers_inst = [b for b in range(n)]

    local = [pltpu.make_async_copy(hid_ref, hbuf.at[t], loc_sem.at[0])]
    own = pl.ds(pl.multiple_of(i * rows, rows), rows)
    local.append(pltpu.make_async_copy(wk_ref, wfull.at[0, own, pl.ds(0, HD)], loc_sem.at[1]))
    local.append(pltpu.make_async_copy(wv_ref, wfull.at[0, own, pl.ds(HD, HD)], loc_sem.at[2]))
    for c in range(1, pieces):
        local.append(
            pltpu.make_async_copy(
                wq_ref.at[:, pl.ds((c - 1) * PIECE, PIECE)], wfull.at[c, own], loc_sem.at[c + 2]
            )
        )
    for copy in local:
        copy.start()

    barrier = pltpu.get_barrier_semaphore()
    for b in peers_inst:

        @pl.when(i != b)
        def _():
            pl.semaphore_signal(barrier, inc=1, device_id=(g, b, t), device_id_type=MESH)

    for other in ((1 - g, i, t), (g, i, t_core), (g, i, t_far)):
        pl.semaphore_signal(barrier, inc=1, device_id=other, device_id_type=MESH)
    pl.semaphore_wait(barrier, n - 1 + 3)

    pending = []

    def start(cond, make):
        pending.append((cond, make))
        if cond is None:
            make().start()
        else:

            @pl.when(cond)
            def _():
                make().start()

    def arrive(cond, make):
        @pl.when(cond)
        def _():
            make().wait_recv()

    def piece(c, j, h):
        return wfull.at[c, pl.ds(pl.multiple_of(j * rows + h * half, half), half)]

    def z_copy(c, d, s, j):
        to = i + 1 if d == 0 else i - 1
        return pltpu.make_async_remote_copy(
            src_ref=piece(c, j, g),
            dst_ref=piece(c, j, g),
            send_sem=z_send.at[c, d, s],
            recv_sem=z_recv.at[c, d, s],
            device_id=(g, to, t),
            device_id_type=MESH,
        )

    def y_copy(c, d, s, j, h):
        return pltpu.make_async_remote_copy(
            src_ref=piece(c, j, h),
            dst_ref=piece(c, j, h),
            send_sem=y_send.at[c, d, s],
            recv_sem=y_recv.at[c, d, s],
            device_id=(1 - g, i, t),
            device_id_type=MESH,
        )

    def hid_copy(k, slot, to):
        return pltpu.make_async_remote_copy(
            src_ref=hbuf.at[slot],
            dst_ref=hbuf.at[slot],
            send_sem=h_send.at[k],
            recv_sem=h_recv.at[k],
            device_id=(g, i, to),
            device_id_type=MESH,
        )

    def send_z(c, s):
        start((i - s >= 0) & (i < n - 1), functools.partial(z_copy, c, 0, s, i - s))
        start((i + s <= n - 1) & (i > 0), functools.partial(z_copy, c, 1, s, i + s))

    def comm(c):
        for s in range(n - 1):
            for d in range(2):
                j = i - 1 - s if d == 0 else i + 1 + s
                have = j >= 0 if d == 0 else j <= n - 1
                arrive(have, functools.partial(z_copy, c, d, s, j))
                if s + 1 < n - 1:
                    onward = have & ((i < n - 1) if d == 0 else (i > 0))
                    start(onward, functools.partial(z_copy, c, d, s + 1, j))
                start(have, functools.partial(y_copy, c, d, s, j, g))

    def settle(c):
        for s in range(n - 1):
            for d in range(2):
                j = i - 1 - s if d == 0 else i + 1 + s
                have = j >= 0 if d == 0 else j <= n - 1
                arrive(have, functools.partial(y_copy, c, d, s, j, 1 - g))

    def norm():
        @pl.loop(0, tokens // 32)
        def _(r):
            here = pl.ds(pl.multiple_of(r * 32, 32), 32)
            total = jnp.zeros((32, 1), jnp.float32)
            for p in range(tp):
                v = hbuf[p, here, :].astype(jnp.float32)
                total = total + jnp.sum(v * v, axis=-1, keepdims=True)
            inverse = lax.rsqrt(total / (tp * part) + NORM_EPS)
            for p in range(tp):
                cols = pl.ds(p * part, part)
                v = hbuf[p, here, :].astype(jnp.float32)
                normed[here, cols] = (v * inverse * gain_ref[:, cols]).astype(jnp.bfloat16)

    def turn(v, here):
        return v * cos_ref[here, :] + pltpu.roll(v, HD // 2, 1) * sin_ref[here, :]

    def product(c):
        @pl.loop(0, tokens // TILE)
        def _(r):
            here = pl.ds(pl.multiple_of(r * TILE, TILE), TILE)
            acc = jnp.dot(normed[here, :], wfull[c], preferred_element_type=jnp.float32)
            acc = acc + bias_ref[:, pl.ds(c * PIECE, PIECE)]
            first, second = acc[:, :HD], acc[:, HD:]
            if c == 0:
                key_ref[here, :] = turn(first, here).astype(jnp.bfloat16)
                val_ref[here, :] = second.astype(jnp.bfloat16)
            else:
                qbuf[here, pl.ds(0, HD)] = turn(first, here).astype(jnp.bfloat16)
                qbuf[here, pl.ds(HD, HD)] = turn(second, here).astype(jnp.bfloat16)

    def attend():
        scale = 1.0 / math.sqrt(HD)
        rr = lax.broadcasted_iota(jnp.int32, (TILE, TILE), 0)
        cc = lax.broadcasted_iota(jnp.int32, (TILE, TILE), 1)
        block = atb.shape[1]
        for r in range(tokens // TILE):
            for head in range(PIECE // HD):
                q = qbuf[pl.ds(r * TILE, TILE), pl.ds(head * HD, HD)]
                width = (r + 1) * TILE
                sc = (
                    lax.dot_general(
                        q,
                        key_ref[pl.ds(0, width), :],
                        (((1,), (1,)), ((), ())),
                        preferred_element_type=jnp.float32,
                    )
                    * scale
                )
                last = jnp.where(rr >= cc, sc[:, width - TILE :], -jnp.inf)
                sc = last if r == 0 else jnp.concatenate([sc[:, : width - TILE], last], axis=1)
                expo = jnp.exp(sc - jnp.max(sc, axis=-1, keepdims=True))
                probs = (expo / jnp.sum(expo, axis=-1, keepdims=True)).astype(jnp.bfloat16)
                mixed = jnp.dot(
                    probs, val_ref[pl.ds(0, width), :], preferred_element_type=jnp.float32
                ).astype(jnp.bfloat16)
                atb[pl.ds(r * (TILE // block), TILE // block), :, pl.ds(head * HD, HD)] = (
                    mixed.reshape(TILE // block, block, HD)
                )

    def d_copy(q, b):
        return pltpu.make_async_remote_copy(
            src_ref=sendbuf.at[q, b],
            dst_ref=got_ref.at[q, i],
            send_sem=d_send.at[q, b],
            recv_sem=d_recv.at[q, i],
            device_id=(g, b, t),
            device_id_type=MESH,
        )

    def d_wait(q, b):
        return pltpu.make_async_remote_copy(
            src_ref=sendbuf.at[q, b],
            dst_ref=got_ref.at[q, b],
            send_sem=d_send.at[q, b],
            recv_sem=d_recv.at[q, b],
            device_id=(g, b, t),
            device_id_type=MESH,
        )

    def stay(q, b):
        return pltpu.make_async_copy(sendbuf.at[q, b], got_ref.at[q, b], d_send.at[q, b])

    def l_copy(b):
        return pltpu.make_async_remote_copy(
            src_ref=lab_ref.at[b],
            dst_ref=lab_out.at[i],
            send_sem=l_send.at[b],
            recv_sem=l_recv.at[i],
            device_id=(g, b, t),
            device_id_type=MESH,
        )

    def l_wait(b):
        return pltpu.make_async_remote_copy(
            src_ref=lab_ref.at[b],
            dst_ref=lab_out.at[b],
            send_sem=l_send.at[b],
            recv_sem=l_recv.at[b],
            device_id=(g, b, t),
            device_id_type=MESH,
        )

    def l_stay(b):
        return pltpu.make_async_copy(lab_ref.at[b], lab_out.at[b], l_send.at[b])

    def dispatch(q):
        for b in peers_inst:
            for k in range(pair):
                sendbuf[q, b, k] = atb[source_ref[b * pair + k]]
            start(i != b, functools.partial(d_copy, q, b))

            @pl.when(i == b)
            def _():
                stay(q, b).start()

    local[0].wait()
    start(None, functools.partial(hid_copy, 0, t, t_far))
    start(None, functools.partial(hid_copy, 1, t, t_core))
    for copy in local[1:]:
        copy.wait()
    send_z(0, 0)
    send_z(1, 0)
    for b in peers_inst:
        start(i != b, functools.partial(l_copy, b))

        @pl.when(i == b)
        def _():
            l_stay(b).start()

    send_z(2, 0)
    comm(0)
    send_z(3, 0)
    comm(1)
    hid_copy(0, t_far, t_far).wait_recv()
    start(None, functools.partial(hid_copy, 2, t_far, t_core))
    send_z(4, 0)
    hid_copy(1, t_core, t_core).wait_recv()
    hid_copy(2, t_diag, t_core).wait_recv()
    norm()
    settle(0)
    product(0)
    comm(2)
    settle(1)
    product(1)
    attend()
    dispatch(0)
    comm(3)
    settle(2)
    product(2)
    comm(4)
    attend()
    dispatch(1)
    settle(3)
    product(3)
    attend()
    dispatch(2)
    settle(4)
    product(4)
    attend()
    dispatch(3)

    for b in peers_inst:

        @pl.when(i != b)
        def _():
            l_wait(b).wait_recv()
            for q in range(pieces - 1):
                d_wait(q, b).wait_recv()

        @pl.when(i == b)
        def _():
            l_stay(b).wait()
            for q in range(pieces - 1):
                stay(q, b).wait()

    for cond, make in pending:
        if cond is None:
            make().wait_send()
        else:

            @pl.when(cond)
            def _():
                make().wait_send()


def fused(
    hidden,
    norm_gain,
    w_query,
    w_key,
    w_value,
    bias_query,
    bias_key,
    bias_value,
    prefix_blocks,
    block_target,
    cache_slot,
):
    owned, block, part = hidden.shape
    n = lax.axis_size("inst")
    tp = lax.axis_size("tp")
    pair = -(-owned // n)
    tokens = owned * block
    slots = jnp.arange(owned, dtype=jnp.int32)
    live = slots < prefix_blocks[0]
    target = block_target[0]
    dest = jnp.where(live, target // BAL, -1)
    place = jnp.where(live, target % BAL, 0)
    earlier = (dest[:, None] == dest[None, :]) & live[None, :] & (slots[None, :] < slots[:, None])
    rank = jnp.sum(earlier.astype(jnp.int32), axis=1)
    item_of_slot = jnp.where(live, dest * pair + rank, -1)
    items = jnp.arange(n * pair, dtype=jnp.int32)
    matched = item_of_slot[None, :] == items[:, None]
    present = jnp.any(matched, axis=1)
    source = jnp.sum(jnp.where(matched, slots[None, :], 0), axis=1)
    item_place = jnp.sum(jnp.where(matched, place[None, :], 0), axis=1)
    label = jnp.where(present, item_place, -1).reshape(n, 1, pair)
    label = jnp.pad(label, ((0, 0), (0, 7), (0, 128 - pair)), constant_values=-1)

    positions = jnp.arange(tokens, dtype=jnp.int32)
    freqs = ROPE_BASE ** (-(jnp.arange(HD // 2, dtype=jnp.float32) * 2.0 / HD))
    angles = positions.astype(jnp.float32)[:, None] * freqs[None, :]
    cosine, sine = jnp.cos(angles), jnp.sin(angles)
    cosine = jnp.concatenate([cosine, cosine], axis=1)
    sine = jnp.concatenate([-sine, sine], axis=1)
    bias = jnp.concatenate([bias_key, bias_value, bias_query])[None, :]

    rows = w_query.shape[0]
    heads_cols = w_query.shape[1]
    pieces = 1 + heads_cols // PIECE
    any_spec = pl.BlockSpec(memory_space=pl.ANY)
    vmem = pl.BlockSpec(memory_space=pltpu.VMEM)
    smem = pl.BlockSpec(memory_space=pltpu.SMEM)
    dma = pltpu.SemaphoreType.DMA
    keys, vals, got, got_label = pl.pallas_call(
        functools.partial(fused_kernel, n, tp, pair),
        out_shape=[
            jax.ShapeDtypeStruct((tokens, HD), jnp.bfloat16),
            jax.ShapeDtypeStruct((tokens, HD), jnp.bfloat16),
            jax.ShapeDtypeStruct((pieces - 1, n, pair, block, PIECE), jnp.bfloat16),
            jax.ShapeDtypeStruct((n, 8, 128), jnp.int32),
        ],
        in_specs=[smem, any_spec, any_spec, any_spec, any_spec, vmem, vmem, vmem, vmem, any_spec],
        out_specs=[vmem, vmem, any_spec, any_spec],
        scratch_shapes=[
            pltpu.VMEM((tp, tokens, part), jnp.bfloat16),
            pltpu.VMEM((tokens, tp * part), jnp.bfloat16),
            pltpu.VMEM((pieces, n * rows, PIECE), jnp.bfloat16),
            pltpu.VMEM((tokens, PIECE), jnp.bfloat16),
            pltpu.VMEM((owned, block, PIECE), jnp.bfloat16),
            pltpu.VMEM((pieces - 1, n, pair, block, PIECE), jnp.bfloat16),
            dma((pieces + 2,)),
            dma((3,)),
            dma((3,)),
            dma((pieces, 2, n - 1)),
            dma((pieces, 2, n - 1)),
            dma((pieces, 2, n - 1)),
            dma((pieces, 2, n - 1)),
            dma((pieces - 1, n)),
            dma((pieces - 1, n)),
            dma((n,)),
            dma((n,)),
        ],
        compiler_params=pltpu.CompilerParams(
            collective_id=0, has_side_effects=True, vmem_limit_bytes=56 * 1024 * 1024
        ),
    )(
        source,
        hidden.reshape(tokens, part),
        w_query,
        w_key,
        w_value,
        norm_gain[None, :],
        bias,
        cosine,
        sine,
        label,
    )

    perm = cache_slot[0]
    inverse = jnp.sum(jnp.where(perm[None, :] == slots[:, None], slots[None, :], 0), axis=1)
    zero_half = jnp.zeros((), jnp.bfloat16)
    live_blocks = (inverse < prefix_blocks[0])[:, None, None]
    keys = keys.reshape(owned, block, -1)
    vals = vals.reshape(owned, block, -1)
    key_cache = jnp.where(live_blocks, jnp.take(keys, inverse, axis=0), zero_half)
    value_cache = jnp.where(live_blocks, jnp.take(vals, inverse, axis=0), zero_half)
    labels = got_label[:, 0, :pair].reshape(-1)
    wanted = labels[None, :] == jnp.arange(BAL, dtype=jnp.int32)[:, None]
    chosen = jnp.sum(jnp.where(wanted, items[None, :], 0), axis=1)
    got = got.reshape(pieces - 1, n * pair, block, PIECE)
    attn_out = jnp.take(got, chosen, axis=1)
    attn_out = jnp.moveaxis(attn_out, 0, 2).reshape(BAL, block, heads_cols)
    return (attn_out, key_cache, value_cache)


def solution(mesh):
    small = mesh.shape["inst"] == 4 and mesh.shape["tp"] == 4 and mesh.shape["groups"] == 2
    in_specs = (
        P(("groups", "inst"), None, "tp"),
        P(),
        P("inst", "tp"),
        P("inst", "tp"),
        P("inst", "tp"),
        P("tp"),
        P("tp"),
        P("tp"),
        P(("groups", "inst")),
        P(("groups", "inst"), None),
        P(("groups", "inst"), None),
    )
    out_specs = (
        P(("groups", "inst"), None, "tp"),
        P(("groups", "inst"), None, "tp"),
        P(("groups", "inst"), None, "tp"),
    )
    body = fused if small else shards
    return jax.shard_map(body, mesh=mesh, in_specs=in_specs, out_specs=out_specs, check_vma=False)
```

```python
import functools
import math

import jax
import jax.numpy as jnp
import numpy as np
from jax import lax
from jax.experimental import pallas as pl
from jax.experimental.pallas import tpu as pltpu
from jax.sharding import PartitionSpec as P

HD = 128
BAL = 12


ROPE_BASE = 1000000.0
NORM_EPS = 1e-06


def rotate(values, positions):
    width = values.shape[-1]
    half = width // 2
    freqs = ROPE_BASE ** (-(jnp.arange(half, dtype=jnp.float32) * 2.0 / width))
    angles = positions.astype(jnp.float32)[:, None] * freqs[None, :]
    cosine = jnp.cos(angles)[:, None, :]
    sine = jnp.sin(angles)[:, None, :]
    first = values[..., :half]
    second = values[..., half:]
    return jnp.concatenate(
        [first * cosine - second * sine, second * cosine + first * sine], axis=-1
    )


def project(whole, positions, norm_gain, w_query, w_key, w_value, bias_query, bias_key, bias_value):
    values = whole.astype(jnp.float32)
    inverse_rms = lax.rsqrt(jnp.mean(values * values, axis=-1, keepdims=True) + NORM_EPS)
    normed = (values * inverse_rms * norm_gain).astype(jnp.bfloat16)
    total_rows = normed.shape[0]
    query_sum = jnp.dot(
        normed,
        lax.all_gather(w_query, "inst", axis=0, tiled=True),
        preferred_element_type=jnp.float32,
    )
    key_sum = jnp.dot(
        normed,
        lax.all_gather(w_key, "inst", axis=0, tiled=True),
        preferred_element_type=jnp.float32,
    )
    value_sum = jnp.dot(
        normed,
        lax.all_gather(w_value, "inst", axis=0, tiled=True),
        preferred_element_type=jnp.float32,
    )
    query = query_sum
    keys = key_sum
    vals = value_sum
    query = rotate((query + bias_query).reshape(total_rows, -1, HD), positions)
    query = query.reshape(total_rows, -1).astype(jnp.bfloat16)
    keys = rotate((keys + bias_key).reshape(total_rows, -1, HD), positions)
    keys = keys.reshape(total_rows, -1).astype(jnp.bfloat16)
    vals = (vals + bias_value).astype(jnp.bfloat16)
    return (query, keys, vals)


def pick_slots(labels_place, labels_live, count):
    items = jnp.arange(labels_place.shape[0], dtype=jnp.int32)
    wanted = (labels_place[None, :] == jnp.arange(count, dtype=jnp.int32)[:, None]) & (
        labels_live[None, :] == 1
    )
    return jnp.sum(jnp.where(wanted, items[None, :], 0), axis=1)


def shards(
    hidden,
    norm_gain,
    w_query,
    w_key,
    w_value,
    bias_query,
    bias_key,
    bias_value,
    prefix_blocks,
    block_target,
    cache_slot,
):
    owned, width_block, part_width = hidden.shape
    peers = lax.axis_size("inst")
    pair = -(-owned // peers)
    total_rows = owned * width_block
    slots = jnp.arange(owned, dtype=jnp.int32)
    live = slots < prefix_blocks[0]
    target = block_target[0]
    dest = jnp.where(live, target // BAL, -1)
    place = jnp.where(live, target % BAL, 0)
    earlier = (dest[:, None] == dest[None, :]) & live[None, :] & (slots[None, :] < slots[:, None])
    rank = jnp.sum(earlier.astype(jnp.int32), axis=1)
    item_of_slot = jnp.where(live, dest * pair + rank, -1)
    items = jnp.arange(peers * pair, dtype=jnp.int32)
    matched = item_of_slot[None, :] == items[:, None]
    present = jnp.any(matched, axis=1)
    source = jnp.sum(jnp.where(matched, slots[None, :], 0), axis=1)
    own_positions = jnp.arange(total_rows, dtype=jnp.int32)
    zero_half = jnp.zeros((), jnp.bfloat16)
    whole = lax.all_gather(hidden.reshape(total_rows, part_width), "tp", axis=1, tiled=True)
    query, keys, vals = project(
        whole, own_positions, norm_gain, w_query, w_key, w_value, bias_query, bias_key, bias_value
    )
    kv_here = keys.shape[1] // HD
    group = query.shape[1] // (HD * kv_here)
    query_heads = query.reshape(total_rows, kv_here, group, HD)
    key_heads = keys.reshape(total_rows, kv_here, HD)
    value_heads = vals.reshape(total_rows, kv_here, HD)
    causal = own_positions[:, None] >= own_positions[None, :]
    scale_factor = 1.0 / math.sqrt(HD)

    def head(query_group):
        scores = (
            jnp.einsum("rkd,skd->krs", query_group, key_heads, preferred_element_type=jnp.float32)
            * scale_factor
        )
        scores = jnp.where(causal[None], scores, -jnp.inf)
        largest = jnp.max(scores, axis=-1, keepdims=True)
        expo = jnp.exp(scores - largest)
        probs = (expo / jnp.sum(expo, axis=-1, keepdims=True)).astype(jnp.bfloat16)
        mixed = jnp.einsum("krs,skd->rkd", probs, value_heads, preferred_element_type=jnp.float32)
        return mixed.astype(jnp.bfloat16)

    heads_out = lax.map(head, jnp.moveaxis(query_heads, 2, 0))
    attention = jnp.transpose(heads_out, (1, 2, 0, 3)).reshape(owned, width_block, -1)
    perm = cache_slot[0]
    inverse = jnp.sum(jnp.where(perm[None, :] == slots[:, None], slots[None, :], 0), axis=1)
    live_blocks = live[:, None, None]
    key_blocks = jnp.where(live_blocks, keys.reshape(owned, width_block, -1), zero_half)
    value_blocks = jnp.where(live_blocks, vals.reshape(owned, width_block, -1), zero_half)
    key_cache = jnp.take(key_blocks, inverse, axis=0)
    value_cache = jnp.take(value_blocks, inverse, axis=0)
    send_out = jnp.where(present[:, None, None], jnp.take(attention, source, axis=0), zero_half)
    send_out = send_out.reshape(peers, pair, width_block, -1)
    out_labels = jnp.stack([jnp.take(place, source), present.astype(jnp.int32)], axis=-1).reshape(
        peers, pair, 2
    )
    got_out, got_out_labels = (
        lax.all_to_all(send_out, "inst", split_axis=0, concat_axis=0, tiled=True),
        lax.all_to_all(out_labels, "inst", split_axis=0, concat_axis=0, tiled=True),
    )
    got_out = got_out.reshape(peers * pair, width_block, -1)
    got_out_labels = got_out_labels.reshape(peers * pair, 2)
    chosen_out = pick_slots(got_out_labels[:, 0], got_out_labels[:, 1], BAL)
    attn_out = jnp.take(got_out, chosen_out, axis=0)
    return (attn_out, key_cache, value_cache)


TILE = 256
PIECE = 256
MESH = pl.DeviceIdType.MESH


def cut(slabs):
    whole = [(k, 0, PIECE) for k in range(slabs - 1)]
    return whole + [(slabs - 1, 0, HD), (slabs - 1, HD, HD)]


def fused_kernel(
    n,
    tp,
    pair,
    source_ref,
    hid_ref,
    wq_ref,
    wk_ref,
    wv_ref,
    gain_ref,
    bias_ref,
    cos_ref,
    sin_ref,
    lab_ref,
    key_ref,
    val_ref,
    got_ref,
    lab_out,
    hbuf,
    normed,
    wfull,
    qbuf,
    atb,
    sendbuf,
    loc_sem,
    h_send,
    h_recv,
    z_send,
    z_recv,
    y_send,
    y_recv,
    d_send,
    d_recv,
    l_send,
    l_recv,
):
    g = lax.axis_index("groups")
    i = lax.axis_index("inst")
    t = lax.axis_index("tp")
    x, core = t // 2, t % 2
    t_core = 2 * x + (1 - core)
    t_far = 2 * (1 - x) + core
    t_diag = 2 * (1 - x) + (1 - core)
    tokens, part = hid_ref.shape
    rows = wq_ref.shape[0]
    half = rows // 2
    parts = cut(wfull.shape[0])
    pieces = len(parts)
    peers_inst = [b for b in range(n)]

    local = [pltpu.make_async_copy(hid_ref, hbuf.at[t], loc_sem.at[0])]
    own = pl.ds(pl.multiple_of(i * rows, rows), rows)
    local.append(pltpu.make_async_copy(wk_ref, wfull.at[0, own, pl.ds(0, HD)], loc_sem.at[1]))
    local.append(pltpu.make_async_copy(wv_ref, wfull.at[0, own, pl.ds(HD, HD)], loc_sem.at[2]))
    for c in range(1, pieces):
        local.append(
            pltpu.make_async_copy(
                wq_ref.at[:, pl.ds((parts[c][0] - 1) * PIECE + parts[c][1], parts[c][2])],
                wfull.at[parts[c][0], own, pl.ds(parts[c][1], parts[c][2])],
                loc_sem.at[c + 2],
            )
        )
    for copy in local:
        copy.start()

    barrier = pltpu.get_barrier_semaphore()
    for b in peers_inst:

        @pl.when(i != b)
        def _():
            pl.semaphore_signal(barrier, inc=1, device_id=(g, b, t), device_id_type=MESH)

    for other in ((1 - g, i, t), (g, i, t_core), (g, i, t_far)):
        pl.semaphore_signal(barrier, inc=1, device_id=other, device_id_type=MESH)
    pl.semaphore_wait(barrier, n - 1 + 3)

    pending = []

    def start(cond, make):
        pending.append((cond, make))
        if cond is None:
            make().start()
        else:

            @pl.when(cond)
            def _():
                make().start()

    def arrive(cond, make):
        @pl.when(cond)
        def _():
            make().wait_recv()

    def piece(c, j, h):
        slab, off, width = parts[c]
        here = pl.ds(pl.multiple_of(j * rows + h * half, half), half)
        return wfull.at[slab, here, pl.ds(off, width)]

    def z_copy(c, d, s, j):
        to = i + 1 if d == 0 else i - 1
        return pltpu.make_async_remote_copy(
            src_ref=piece(c, j, g),
            dst_ref=piece(c, j, g),
            send_sem=z_send.at[c, d, s],
            recv_sem=z_recv.at[c, d, s],
            device_id=(g, to, t),
            device_id_type=MESH,
        )

    def y_copy(c, d, s, j, h):
        return pltpu.make_async_remote_copy(
            src_ref=piece(c, j, h),
            dst_ref=piece(c, j, h),
            send_sem=y_send.at[c, d, s],
            recv_sem=y_recv.at[c, d, s],
            device_id=(1 - g, i, t),
            device_id_type=MESH,
        )

    def hid_copy(k, slot, to):
        return pltpu.make_async_remote_copy(
            src_ref=hbuf.at[slot],
            dst_ref=hbuf.at[slot],
            send_sem=h_send.at[k],
            recv_sem=h_recv.at[k],
            device_id=(g, i, to),
            device_id_type=MESH,
        )

    def send_z(c, s):
        start((i - s >= 0) & (i < n - 1), functools.partial(z_copy, c, 0, s, i - s))
        start((i + s <= n - 1) & (i > 0), functools.partial(z_copy, c, 1, s, i + s))

    def comm(c, s):
        for d in range(2):
            j = i - 1 - s if d == 0 else i + 1 + s
            have = j >= 0 if d == 0 else j <= n - 1
            arrive(have, functools.partial(z_copy, c, d, s, j))
            if s + 1 < n - 1:
                onward = have & ((i < n - 1) if d == 0 else (i > 0))
                start(onward, functools.partial(z_copy, c, d, s + 1, j))
            start(have, functools.partial(y_copy, c, d, s, j, g))

    def settle(c):
        for s in range(n - 1):
            for d in range(2):
                j = i - 1 - s if d == 0 else i + 1 + s
                have = j >= 0 if d == 0 else j <= n - 1
                arrive(have, functools.partial(y_copy, c, d, s, j, 1 - g))

    def norm():
        @pl.loop(0, tokens // 32)
        def _(r):
            here = pl.ds(pl.multiple_of(r * 32, 32), 32)
            total = jnp.zeros((32, 1), jnp.float32)
            for p in range(tp):
                v = hbuf[p, here, :].astype(jnp.float32)
                total = total + jnp.sum(v * v, axis=-1, keepdims=True)
            inverse = lax.rsqrt(total / (tp * part) + NORM_EPS)
            for p in range(tp):
                cols = pl.ds(p * part, part)
                v = hbuf[p, here, :].astype(jnp.float32)
                normed[here, cols] = (v * inverse * gain_ref[:, cols]).astype(jnp.bfloat16)

    def turn(v, here):
        return v * cos_ref[here, :] + pltpu.roll(v, HD // 2, 1) * sin_ref[here, :]

    def product(c):
        settle(c)
        slab, off, width = parts[c]

        @pl.loop(0, tokens // TILE)
        def _(r):
            here = pl.ds(pl.multiple_of(r * TILE, TILE), TILE)
            acc = jnp.dot(
                normed[here, :],
                wfull[slab, :, pl.ds(off, width)],
                preferred_element_type=jnp.float32,
            )
            acc = acc + bias_ref[:, pl.ds(slab * PIECE + off, width)]
            if c == 0:
                key_ref[here, :] = turn(acc[:, :HD], here).astype(jnp.bfloat16)
                val_ref[here, :] = acc[:, HD:].astype(jnp.bfloat16)
            else:
                for head in range(width // HD):
                    cols = slice(head * HD, (head + 1) * HD)
                    qbuf[here, cols] = turn(acc[:, cols], here).astype(jnp.bfloat16)

    def attend(c):
        scale = 1.0 / math.sqrt(HD)
        rr = lax.broadcasted_iota(jnp.int32, (TILE, TILE), 0)
        cc = lax.broadcasted_iota(jnp.int32, (TILE, TILE), 1)
        block = atb.shape[1]
        for r in range(tokens // TILE):
            for head in range(parts[c][2] // HD):
                q = qbuf[pl.ds(r * TILE, TILE), pl.ds(head * HD, HD)]
                width = (r + 1) * TILE
                sc = (
                    lax.dot_general(
                        q,
                        key_ref[pl.ds(0, width), :],
                        (((1,), (1,)), ((), ())),
                        preferred_element_type=jnp.float32,
                    )
                    * scale
                )
                last = jnp.where(rr >= cc, sc[:, width - TILE :], -jnp.inf)
                sc = last if r == 0 else jnp.concatenate([sc[:, : width - TILE], last], axis=1)
                expo = jnp.exp(sc - jnp.max(sc, axis=-1, keepdims=True))
                probs = (expo / jnp.sum(expo, axis=-1, keepdims=True)).astype(jnp.bfloat16)
                mixed = jnp.dot(
                    probs, val_ref[pl.ds(0, width), :], preferred_element_type=jnp.float32
                ).astype(jnp.bfloat16)
                atb[pl.ds(r * (TILE // block), TILE // block), :, pl.ds(head * HD, HD)] = (
                    mixed.reshape(TILE // block, block, HD)
                )

    def packed(q, b):
        slab, off, width = parts[q + 1]
        return sendbuf.at[slab - 1, b, :, :, pl.ds(off, width)]

    def landed(q, b):
        slab, off, width = parts[q + 1]
        return got_ref.at[slab - 1, b, :, :, pl.ds(off, width)]

    def d_copy(q, b):
        return pltpu.make_async_remote_copy(
            src_ref=packed(q, b),
            dst_ref=landed(q, i),
            send_sem=d_send.at[q, b],
            recv_sem=d_recv.at[q, i],
            device_id=(g, b, t),
            device_id_type=MESH,
        )

    def d_wait(q, b):
        return pltpu.make_async_remote_copy(
            src_ref=packed(q, b),
            dst_ref=landed(q, b),
            send_sem=d_send.at[q, b],
            recv_sem=d_recv.at[q, b],
            device_id=(g, b, t),
            device_id_type=MESH,
        )

    def stay(q, b):
        return pltpu.make_async_copy(packed(q, b), landed(q, b), d_send.at[q, b])

    def l_copy(b):
        return pltpu.make_async_remote_copy(
            src_ref=lab_ref.at[b],
            dst_ref=lab_out.at[i],
            send_sem=l_send.at[b],
            recv_sem=l_recv.at[i],
            device_id=(g, b, t),
            device_id_type=MESH,
        )

    def l_wait(b):
        return pltpu.make_async_remote_copy(
            src_ref=lab_ref.at[b],
            dst_ref=lab_out.at[b],
            send_sem=l_send.at[b],
            recv_sem=l_recv.at[b],
            device_id=(g, b, t),
            device_id_type=MESH,
        )

    def l_stay(b):
        return pltpu.make_async_copy(lab_ref.at[b], lab_out.at[b], l_send.at[b])

    def dispatch(q):
        slab, off, width = parts[q + 1]
        for b in peers_inst:
            for k in range(pair):
                sendbuf[slab - 1, b, k, :, pl.ds(off, width)] = atb[
                    source_ref[b * pair + k], :, pl.ds(0, width)
                ]
            start(i != b, functools.partial(d_copy, q, b))

            @pl.when(i == b)
            def _():
                stay(q, b).start()

    local[0].wait()
    start(None, functools.partial(hid_copy, 0, t, t_far))
    start(None, functools.partial(hid_copy, 1, t, t_core))
    for copy in local[1:]:
        copy.wait()
    send_z(0, 0)
    send_z(1, 0)
    for b in peers_inst:
        start(i != b, functools.partial(l_copy, b))

        @pl.when(i == b)
        def _():
            l_stay(b).start()

    send_z(2, 0)
    last = n - 1

    def comms(c, first=0):
        for s in range(first, last):
            comm(c, s)

    comms(0)
    send_z(3, 0)
    comms(1)
    hid_copy(0, t_far, t_far).wait_recv()
    start(None, functools.partial(hid_copy, 2, t_far, t_core))
    for c in range(4, pieces):
        send_z(c, 0)
    hid_copy(1, t_core, t_core).wait_recv()
    hid_copy(2, t_diag, t_core).wait_recv()
    norm()
    comm(2, 0)
    product(0)
    comms(2, 1)
    for c in range(1, pieces):
        ahead = c + 2
        if ahead < pieces:
            comm(ahead, 0)
        product(c)
        if ahead < pieces:
            comm(ahead, 1)
        attend(c)
        dispatch(c - 1)
        if ahead < pieces:
            comms(ahead, 2)

    for b in peers_inst:

        @pl.when(i != b)
        def _():
            l_wait(b).wait_recv()
            for q in range(pieces - 1):
                d_wait(q, b).wait_recv()

        @pl.when(i == b)
        def _():
            l_stay(b).wait()
            for q in range(pieces - 1):
                stay(q, b).wait()

    for cond, make in pending:
        if cond is None:
            make().wait_send()
        else:

            @pl.when(cond)
            def _():
                make().wait_send()


def fused(
    hidden,
    norm_gain,
    w_query,
    w_key,
    w_value,
    bias_query,
    bias_key,
    bias_value,
    prefix_blocks,
    block_target,
    cache_slot,
):
    owned, block, part = hidden.shape
    n = lax.axis_size("inst")
    tp = lax.axis_size("tp")
    pair = -(-owned // n)
    tokens = owned * block
    slots = jnp.arange(owned, dtype=jnp.int32)
    live = slots < prefix_blocks[0]
    target = block_target[0]
    dest = jnp.where(live, target // BAL, -1)
    place = jnp.where(live, target % BAL, 0)
    earlier = (dest[:, None] == dest[None, :]) & live[None, :] & (slots[None, :] < slots[:, None])
    rank = jnp.sum(earlier.astype(jnp.int32), axis=1)
    item_of_slot = jnp.where(live, dest * pair + rank, -1)
    items = jnp.arange(n * pair, dtype=jnp.int32)
    matched = item_of_slot[None, :] == items[:, None]
    present = jnp.any(matched, axis=1)
    source = jnp.sum(jnp.where(matched, slots[None, :], 0), axis=1)
    item_place = jnp.sum(jnp.where(matched, place[None, :], 0), axis=1)
    label = jnp.where(present, item_place, -1).reshape(n, 1, pair)
    label = jnp.pad(label, ((0, 0), (0, 7), (0, 128 - pair)), constant_values=-1)

    base, power = np.float32(ROPE_BASE), np.arange(HD // 2, dtype=np.float32) * np.float32(2.0 / HD)
    freqs = np.power(base, -power).astype(np.float32)
    angles = np.arange(tokens, dtype=np.float32)[:, None] * freqs[None, :]
    cosine, sine = np.cos(angles), np.sin(angles)
    cosine = jnp.asarray(np.concatenate([cosine, cosine], axis=1))
    sine = jnp.asarray(np.concatenate([-sine, sine], axis=1))
    bias = jnp.concatenate([bias_key, bias_value, bias_query])[None, :]

    rows = w_query.shape[0]
    heads_cols = w_query.shape[1]
    slabs = 1 + heads_cols // PIECE
    pieces = len(cut(slabs))
    any_spec = pl.BlockSpec(memory_space=pl.ANY)
    vmem = pl.BlockSpec(memory_space=pltpu.VMEM)
    smem = pl.BlockSpec(memory_space=pltpu.SMEM)
    dma = pltpu.SemaphoreType.DMA
    keys, vals, got, got_label = pl.pallas_call(
        functools.partial(fused_kernel, n, tp, pair),
        out_shape=[
            jax.ShapeDtypeStruct((tokens, HD), jnp.bfloat16),
            jax.ShapeDtypeStruct((tokens, HD), jnp.bfloat16),
            jax.ShapeDtypeStruct((slabs - 1, n, pair, block, PIECE), jnp.bfloat16),
            jax.ShapeDtypeStruct((n, 8, 128), jnp.int32),
        ],
        in_specs=[smem, any_spec, any_spec, any_spec, any_spec, vmem, vmem, vmem, vmem, any_spec],
        out_specs=[vmem, vmem, any_spec, any_spec],
        scratch_shapes=[
            pltpu.VMEM((tp, tokens, part), jnp.bfloat16),
            pltpu.VMEM((tokens, tp * part), jnp.bfloat16),
            pltpu.VMEM((slabs, n * rows, PIECE), jnp.bfloat16),
            pltpu.VMEM((tokens, PIECE), jnp.bfloat16),
            pltpu.VMEM((owned, block, PIECE), jnp.bfloat16),
            pltpu.VMEM((slabs - 1, n, pair, block, PIECE), jnp.bfloat16),
            dma((pieces + 2,)),
            dma((3,)),
            dma((3,)),
            dma((pieces, 2, n - 1)),
            dma((pieces, 2, n - 1)),
            dma((pieces, 2, n - 1)),
            dma((pieces, 2, n - 1)),
            dma((pieces - 1, n)),
            dma((pieces - 1, n)),
            dma((n,)),
            dma((n,)),
        ],
        compiler_params=pltpu.CompilerParams(
            collective_id=0, has_side_effects=True, vmem_limit_bytes=56 * 1024 * 1024
        ),
    )(
        source,
        hidden.reshape(tokens, part),
        w_query,
        w_key,
        w_value,
        norm_gain[None, :],
        bias,
        cosine,
        sine,
        label,
    )

    perm = cache_slot[0]
    inverse = jnp.sum(jnp.where(perm[None, :] == slots[:, None], slots[None, :], 0), axis=1)
    zero_half = jnp.zeros((), jnp.bfloat16)
    live_blocks = (inverse < prefix_blocks[0])[:, None, None]
    keys = keys.reshape(owned, block, -1)
    vals = vals.reshape(owned, block, -1)
    key_cache = jnp.where(live_blocks, jnp.take(keys, inverse, axis=0), zero_half)
    value_cache = jnp.where(live_blocks, jnp.take(vals, inverse, axis=0), zero_half)
    labels = got_label[:, 0, :pair].reshape(-1)
    wanted = labels[None, :] == jnp.arange(BAL, dtype=jnp.int32)[:, None]
    chosen = jnp.sum(jnp.where(wanted, items[None, :], 0), axis=1)
    got = got.reshape(slabs - 1, n * pair, block, PIECE)
    attn_out = jnp.take(got, chosen, axis=1)
    attn_out = jnp.moveaxis(attn_out, 0, 2).reshape(BAL, block, heads_cols)
    return (attn_out, key_cache, value_cache)


def solution(mesh):
    small = mesh.shape["inst"] == 4 and mesh.shape["tp"] == 4 and mesh.shape["groups"] == 2
    in_specs = (
        P(("groups", "inst"), None, "tp"),
        P(),
        P("inst", "tp"),
        P("inst", "tp"),
        P("inst", "tp"),
        P("tp"),
        P("tp"),
        P("tp"),
        P(("groups", "inst")),
        P(("groups", "inst"), None),
        P(("groups", "inst"), None),
    )
    out_specs = (
        P(("groups", "inst"), None, "tp"),
        P(("groups", "inst"), None, "tp"),
        P(("groups", "inst"), None, "tp"),
    )
    body = fused if small else shards
    return jax.shard_map(body, mesh=mesh, in_specs=in_specs, out_specs=out_specs, check_vma=False)
```

```python
import functools
import math

import jax
import jax.numpy as jnp
import numpy as np
from jax import lax
from jax.experimental import pallas as pl
from jax.experimental.pallas import tpu as pltpu
from jax.sharding import PartitionSpec as P

HD = 128
BAL = 12


ROPE_BASE = 1000000.0
NORM_EPS = 1e-06


def rotate(values, positions):
    width = values.shape[-1]
    half = width // 2
    freqs = ROPE_BASE ** (-(jnp.arange(half, dtype=jnp.float32) * 2.0 / width))
    angles = positions.astype(jnp.float32)[:, None] * freqs[None, :]
    cosine = jnp.cos(angles)[:, None, :]
    sine = jnp.sin(angles)[:, None, :]
    first = values[..., :half]
    second = values[..., half:]
    return jnp.concatenate(
        [first * cosine - second * sine, second * cosine + first * sine], axis=-1
    )


def project(whole, positions, norm_gain, w_query, w_key, w_value, bias_query, bias_key, bias_value):
    values = whole.astype(jnp.float32)
    inverse_rms = lax.rsqrt(jnp.mean(values * values, axis=-1, keepdims=True) + NORM_EPS)
    normed = (values * inverse_rms * norm_gain).astype(jnp.bfloat16)
    total_rows = normed.shape[0]
    query_sum = jnp.dot(
        normed,
        lax.all_gather(w_query, "inst", axis=0, tiled=True),
        preferred_element_type=jnp.float32,
    )
    key_sum = jnp.dot(
        normed,
        lax.all_gather(w_key, "inst", axis=0, tiled=True),
        preferred_element_type=jnp.float32,
    )
    value_sum = jnp.dot(
        normed,
        lax.all_gather(w_value, "inst", axis=0, tiled=True),
        preferred_element_type=jnp.float32,
    )
    query = query_sum
    keys = key_sum
    vals = value_sum
    query = rotate((query + bias_query).reshape(total_rows, -1, HD), positions)
    query = query.reshape(total_rows, -1).astype(jnp.bfloat16)
    keys = rotate((keys + bias_key).reshape(total_rows, -1, HD), positions)
    keys = keys.reshape(total_rows, -1).astype(jnp.bfloat16)
    vals = (vals + bias_value).astype(jnp.bfloat16)
    return (query, keys, vals)


def pick_slots(labels_place, labels_live, count):
    items = jnp.arange(labels_place.shape[0], dtype=jnp.int32)
    wanted = (labels_place[None, :] == jnp.arange(count, dtype=jnp.int32)[:, None]) & (
        labels_live[None, :] == 1
    )
    return jnp.sum(jnp.where(wanted, items[None, :], 0), axis=1)


def shards(
    hidden,
    norm_gain,
    w_query,
    w_key,
    w_value,
    bias_query,
    bias_key,
    bias_value,
    prefix_blocks,
    block_target,
    cache_slot,
):
    owned, width_block, part_width = hidden.shape
    peers = lax.axis_size("inst")
    pair = -(-owned // peers)
    total_rows = owned * width_block
    slots = jnp.arange(owned, dtype=jnp.int32)
    live = slots < prefix_blocks[0]
    target = block_target[0]
    dest = jnp.where(live, target // BAL, -1)
    place = jnp.where(live, target % BAL, 0)
    earlier = (dest[:, None] == dest[None, :]) & live[None, :] & (slots[None, :] < slots[:, None])
    rank = jnp.sum(earlier.astype(jnp.int32), axis=1)
    item_of_slot = jnp.where(live, dest * pair + rank, -1)
    items = jnp.arange(peers * pair, dtype=jnp.int32)
    matched = item_of_slot[None, :] == items[:, None]
    present = jnp.any(matched, axis=1)
    source = jnp.sum(jnp.where(matched, slots[None, :], 0), axis=1)
    own_positions = jnp.arange(total_rows, dtype=jnp.int32)
    zero_half = jnp.zeros((), jnp.bfloat16)
    whole = lax.all_gather(hidden.reshape(total_rows, part_width), "tp", axis=1, tiled=True)
    query, keys, vals = project(
        whole, own_positions, norm_gain, w_query, w_key, w_value, bias_query, bias_key, bias_value
    )
    kv_here = keys.shape[1] // HD
    group = query.shape[1] // (HD * kv_here)
    query_heads = query.reshape(total_rows, kv_here, group, HD)
    key_heads = keys.reshape(total_rows, kv_here, HD)
    value_heads = vals.reshape(total_rows, kv_here, HD)
    causal = own_positions[:, None] >= own_positions[None, :]
    scale_factor = 1.0 / math.sqrt(HD)

    def head(query_group):
        scores = (
            jnp.einsum("rkd,skd->krs", query_group, key_heads, preferred_element_type=jnp.float32)
            * scale_factor
        )
        scores = jnp.where(causal[None], scores, -jnp.inf)
        largest = jnp.max(scores, axis=-1, keepdims=True)
        expo = jnp.exp(scores - largest)
        probs = (expo / jnp.sum(expo, axis=-1, keepdims=True)).astype(jnp.bfloat16)
        mixed = jnp.einsum("krs,skd->rkd", probs, value_heads, preferred_element_type=jnp.float32)
        return mixed.astype(jnp.bfloat16)

    heads_out = lax.map(head, jnp.moveaxis(query_heads, 2, 0))
    attention = jnp.transpose(heads_out, (1, 2, 0, 3)).reshape(owned, width_block, -1)
    perm = cache_slot[0]
    inverse = jnp.sum(jnp.where(perm[None, :] == slots[:, None], slots[None, :], 0), axis=1)
    live_blocks = live[:, None, None]
    key_blocks = jnp.where(live_blocks, keys.reshape(owned, width_block, -1), zero_half)
    value_blocks = jnp.where(live_blocks, vals.reshape(owned, width_block, -1), zero_half)
    key_cache = jnp.take(key_blocks, inverse, axis=0)
    value_cache = jnp.take(value_blocks, inverse, axis=0)
    send_out = jnp.where(present[:, None, None], jnp.take(attention, source, axis=0), zero_half)
    send_out = send_out.reshape(peers, pair, width_block, -1)
    out_labels = jnp.stack([jnp.take(place, source), present.astype(jnp.int32)], axis=-1).reshape(
        peers, pair, 2
    )
    got_out, got_out_labels = (
        lax.all_to_all(send_out, "inst", split_axis=0, concat_axis=0, tiled=True),
        lax.all_to_all(out_labels, "inst", split_axis=0, concat_axis=0, tiled=True),
    )
    got_out = got_out.reshape(peers * pair, width_block, -1)
    got_out_labels = got_out_labels.reshape(peers * pair, 2)
    chosen_out = pick_slots(got_out_labels[:, 0], got_out_labels[:, 1], BAL)
    attn_out = jnp.take(got_out, chosen_out, axis=0)
    return (attn_out, key_cache, value_cache)


TILE = 256
PIECE = 256
MESH = pl.DeviceIdType.MESH


def cut(slabs):
    whole = [(k, 0, PIECE) for k in range(slabs - 1)]
    return whole + [(slabs - 1, 0, HD), (slabs - 1, HD, HD)]


def fused_kernel(
    n,
    tp,
    pair,
    source_ref,
    hid_ref,
    wq_ref,
    wk_ref,
    wv_ref,
    gain_ref,
    bias_ref,
    cos_ref,
    sin_ref,
    lab_ref,
    key_ref,
    val_ref,
    got_ref,
    lab_out,
    hbuf,
    normed,
    wfull,
    qbuf,
    atb,
    sendbuf,
    loc_sem,
    h_send,
    h_recv,
    z_send,
    z_recv,
    y_send,
    y_recv,
    d_send,
    d_recv,
    l_send,
    l_recv,
):
    g = lax.axis_index("groups")
    i = lax.axis_index("inst")
    t = lax.axis_index("tp")
    x, core = t // 2, t % 2
    t_core = 2 * x + (1 - core)
    t_far = 2 * (1 - x) + core
    t_diag = 2 * (1 - x) + (1 - core)
    tokens, part = hid_ref.shape
    rows = wq_ref.shape[0]
    half = rows // 2
    parts = cut(wfull.shape[0])
    pieces = len(parts)
    peers_inst = [b for b in range(n)]

    local = [pltpu.make_async_copy(hid_ref, hbuf.at[t], loc_sem.at[0])]
    own = pl.ds(pl.multiple_of(i * rows, rows), rows)
    local.append(pltpu.make_async_copy(wk_ref, wfull.at[0, own, pl.ds(0, HD)], loc_sem.at[1]))
    local.append(pltpu.make_async_copy(wv_ref, wfull.at[0, own, pl.ds(HD, HD)], loc_sem.at[2]))
    for c in range(1, pieces):
        local.append(
            pltpu.make_async_copy(
                wq_ref.at[:, pl.ds((parts[c][0] - 1) * PIECE + parts[c][1], parts[c][2])],
                wfull.at[parts[c][0], own, pl.ds(parts[c][1], parts[c][2])],
                loc_sem.at[c + 2],
            )
        )
    for copy in local[1:3] + local[:1] + local[3:]:
        copy.start()

    barrier = pltpu.get_barrier_semaphore()
    for b in peers_inst:

        @pl.when(i != b)
        def _():
            pl.semaphore_signal(barrier, inc=1, device_id=(g, b, t), device_id_type=MESH)

    for other in ((1 - g, i, t), (g, i, t_core), (g, i, t_far)):
        pl.semaphore_signal(barrier, inc=1, device_id=other, device_id_type=MESH)
    pl.semaphore_wait(barrier, n - 1 + 3)

    pending = []

    def start(cond, make):
        pending.append((cond, make))
        if cond is None:
            make().start()
        else:

            @pl.when(cond)
            def _():
                make().start()

    def arrive(cond, make):
        @pl.when(cond)
        def _():
            make().wait_recv()

    def piece(c, j, h):
        slab, off, width = parts[c]
        here = pl.ds(pl.multiple_of(j * rows + h * half, half), half)
        return wfull.at[slab, here, pl.ds(off, width)]

    def z_copy(c, d, s, j):
        to = i + 1 if d == 0 else i - 1
        return pltpu.make_async_remote_copy(
            src_ref=piece(c, j, g),
            dst_ref=piece(c, j, g),
            send_sem=z_send.at[c, d, s],
            recv_sem=z_recv.at[c, d, s],
            device_id=(g, to, t),
            device_id_type=MESH,
        )

    def y_copy(c, d, s, j, h):
        return pltpu.make_async_remote_copy(
            src_ref=piece(c, j, h),
            dst_ref=piece(c, j, h),
            send_sem=y_send.at[c, d, s],
            recv_sem=y_recv.at[c, d, s],
            device_id=(1 - g, i, t),
            device_id_type=MESH,
        )

    def hid_copy(k, slot, to):
        return pltpu.make_async_remote_copy(
            src_ref=hbuf.at[slot],
            dst_ref=hbuf.at[slot],
            send_sem=h_send.at[k],
            recv_sem=h_recv.at[k],
            device_id=(g, i, to),
            device_id_type=MESH,
        )

    def send_z(c, s):
        start((i - s >= 0) & (i < n - 1), functools.partial(z_copy, c, 0, s, i - s))
        start((i + s <= n - 1) & (i > 0), functools.partial(z_copy, c, 1, s, i + s))

    def comm(c, s):
        for d in range(2):
            j = i - 1 - s if d == 0 else i + 1 + s
            have = j >= 0 if d == 0 else j <= n - 1
            arrive(have, functools.partial(z_copy, c, d, s, j))
            if s + 1 < n - 1:
                onward = have & ((i < n - 1) if d == 0 else (i > 0))
                start(onward, functools.partial(z_copy, c, d, s + 1, j))
            start(have, functools.partial(y_copy, c, d, s, j, g))

    def settle(c):
        for s in range(n - 1):
            for d in range(2):
                j = i - 1 - s if d == 0 else i + 1 + s
                have = j >= 0 if d == 0 else j <= n - 1
                arrive(have, functools.partial(y_copy, c, d, s, j, 1 - g))

    def norm():
        @pl.loop(0, tokens // 32)
        def _(r):
            here = pl.ds(pl.multiple_of(r * 32, 32), 32)
            total = jnp.zeros((32, 1), jnp.float32)
            for p in range(tp):
                v = hbuf[p, here, :].astype(jnp.float32)
                total = total + jnp.sum(v * v, axis=-1, keepdims=True)
            inverse = lax.rsqrt(total / (tp * part) + NORM_EPS)
            for p in range(tp):
                cols = pl.ds(p * part, part)
                v = hbuf[p, here, :].astype(jnp.float32)
                normed[here, cols] = (v * inverse * gain_ref[:, cols]).astype(jnp.bfloat16)

    def turn(v, here):
        return v * cos_ref[here, :] + pltpu.roll(v, HD // 2, 1) * sin_ref[here, :]

    def product(c):
        settle(c)
        slab, off, width = parts[c]

        @pl.loop(0, tokens // TILE)
        def _(r):
            here = pl.ds(pl.multiple_of(r * TILE, TILE), TILE)
            acc = jnp.dot(
                normed[here, :],
                wfull[slab, :, pl.ds(off, width)],
                preferred_element_type=jnp.float32,
            )
            acc = acc + bias_ref[:, pl.ds(slab * PIECE + off, width)]
            if c == 0:
                key_ref[here, :] = turn(acc[:, :HD], here).astype(jnp.bfloat16)
                val_ref[here, :] = acc[:, HD:].astype(jnp.bfloat16)
            else:
                for head in range(width // HD):
                    cols = slice(head * HD, (head + 1) * HD)
                    qbuf[here, cols] = turn(acc[:, cols], here).astype(jnp.bfloat16)

    def attend(c):
        scale = 1.0 / math.sqrt(HD)
        rr = lax.broadcasted_iota(jnp.int32, (TILE, TILE), 0)
        cc = lax.broadcasted_iota(jnp.int32, (TILE, TILE), 1)
        block = atb.shape[1]
        for r in range(tokens // TILE):
            for head in range(parts[c][2] // HD):
                q = qbuf[pl.ds(r * TILE, TILE), pl.ds(head * HD, HD)]
                width = (r + 1) * TILE
                sc = (
                    lax.dot_general(
                        q,
                        key_ref[pl.ds(0, width), :],
                        (((1,), (1,)), ((), ())),
                        preferred_element_type=jnp.float32,
                    )
                    * scale
                )
                last = jnp.where(rr >= cc, sc[:, width - TILE :], -jnp.inf)
                sc = last if r == 0 else jnp.concatenate([sc[:, : width - TILE], last], axis=1)
                expo = jnp.exp(sc - jnp.max(sc, axis=-1, keepdims=True))
                probs = (expo / jnp.sum(expo, axis=-1, keepdims=True)).astype(jnp.bfloat16)
                mixed = jnp.dot(
                    probs, val_ref[pl.ds(0, width), :], preferred_element_type=jnp.float32
                ).astype(jnp.bfloat16)
                atb[pl.ds(r * (TILE // block), TILE // block), :, pl.ds(head * HD, HD)] = (
                    mixed.reshape(TILE // block, block, HD)
                )

    def packed(q, b):
        slab, off, width = parts[q + 1]
        return sendbuf.at[slab - 1, b, :, :, pl.ds(off, width)]

    def landed(q, b):
        slab, off, width = parts[q + 1]
        return got_ref.at[slab - 1, b, :, :, pl.ds(off, width)]

    def d_copy(q, b):
        return pltpu.make_async_remote_copy(
            src_ref=packed(q, b),
            dst_ref=landed(q, i),
            send_sem=d_send.at[q, b],
            recv_sem=d_recv.at[q, i],
            device_id=(g, b, t),
            device_id_type=MESH,
        )

    def d_wait(q, b):
        return pltpu.make_async_remote_copy(
            src_ref=packed(q, b),
            dst_ref=landed(q, b),
            send_sem=d_send.at[q, b],
            recv_sem=d_recv.at[q, b],
            device_id=(g, b, t),
            device_id_type=MESH,
        )

    def stay(q, b):
        return pltpu.make_async_copy(packed(q, b), landed(q, b), d_send.at[q, b])

    def l_copy(b):
        return pltpu.make_async_remote_copy(
            src_ref=lab_ref.at[b],
            dst_ref=lab_out.at[i],
            send_sem=l_send.at[b],
            recv_sem=l_recv.at[i],
            device_id=(g, b, t),
            device_id_type=MESH,
        )

    def l_wait(b):
        return pltpu.make_async_remote_copy(
            src_ref=lab_ref.at[b],
            dst_ref=lab_out.at[b],
            send_sem=l_send.at[b],
            recv_sem=l_recv.at[b],
            device_id=(g, b, t),
            device_id_type=MESH,
        )

    def l_stay(b):
        return pltpu.make_async_copy(lab_ref.at[b], lab_out.at[b], l_send.at[b])

    def dispatch(q):
        slab, off, width = parts[q + 1]
        for b in peers_inst:
            for k in range(pair):
                sendbuf[slab - 1, b, k, :, pl.ds(off, width)] = atb[
                    source_ref[b * pair + k], :, pl.ds(0, width)
                ]
            start(i != b, functools.partial(d_copy, q, b))

            @pl.when(i == b)
            def _():
                stay(q, b).start()

    local[1].wait()
    local[2].wait()
    send_z(0, 0)
    local[0].wait()
    start(None, functools.partial(hid_copy, 0, t, t_far))
    start(None, functools.partial(hid_copy, 1, t, t_core))
    for copy in local[3:]:
        copy.wait()
    send_z(1, 0)
    for b in peers_inst:
        start(i != b, functools.partial(l_copy, b))

        @pl.when(i == b)
        def _():
            l_stay(b).start()

    send_z(2, 0)
    last = n - 1

    def comms(c, first=0):
        for s in range(first, last):
            comm(c, s)

    comms(0)
    send_z(3, 0)
    comms(1)
    hid_copy(0, t_far, t_far).wait_recv()
    start(None, functools.partial(hid_copy, 2, t_far, t_core))
    for c in range(4, pieces):
        send_z(c, 0)
    hid_copy(1, t_core, t_core).wait_recv()
    hid_copy(2, t_diag, t_core).wait_recv()
    norm()
    comm(2, 0)
    product(0)
    comms(2, 1)
    for c in range(1, pieces):
        ahead = c + 2
        if ahead < pieces:
            comm(ahead, 0)
        product(c)
        if ahead == pieces:
            comms(ahead - 1, 2)
        elif ahead < pieces - 1:
            comm(ahead, 1)
        attend(c)
        dispatch(c - 1)
        if ahead < pieces - 1:
            comms(ahead, 2)
        elif ahead == pieces - 1:
            comm(ahead, 1)

    for b in peers_inst:

        @pl.when(i != b)
        def _():
            l_wait(b).wait_recv()
            for q in range(pieces - 1):
                d_wait(q, b).wait_recv()

        @pl.when(i == b)
        def _():
            l_stay(b).wait()
            for q in range(pieces - 1):
                stay(q, b).wait()

    for cond, make in pending:
        if cond is None:
            make().wait_send()
        else:

            @pl.when(cond)
            def _():
                make().wait_send()


def fused(
    hidden,
    norm_gain,
    w_query,
    w_key,
    w_value,
    bias_query,
    bias_key,
    bias_value,
    prefix_blocks,
    block_target,
    cache_slot,
):
    owned, block, part = hidden.shape
    n = lax.axis_size("inst")
    tp = lax.axis_size("tp")
    pair = -(-owned // n)
    tokens = owned * block
    slots = jnp.arange(owned, dtype=jnp.int32)
    live = slots < prefix_blocks[0]
    target = block_target[0]
    dest = jnp.where(live, target // BAL, -1)
    place = jnp.where(live, target % BAL, 0)
    earlier = (dest[:, None] == dest[None, :]) & live[None, :] & (slots[None, :] < slots[:, None])
    rank = jnp.sum(earlier.astype(jnp.int32), axis=1)
    item_of_slot = jnp.where(live, dest * pair + rank, -1)
    items = jnp.arange(n * pair, dtype=jnp.int32)
    matched = item_of_slot[None, :] == items[:, None]
    present = jnp.any(matched, axis=1)
    source = jnp.sum(jnp.where(matched, slots[None, :], 0), axis=1)
    item_place = jnp.sum(jnp.where(matched, place[None, :], 0), axis=1)
    label = jnp.where(present, item_place, -1).reshape(n, 1, pair)
    label = jnp.pad(label, ((0, 0), (0, 7), (0, 128 - pair)), constant_values=-1)

    base, power = np.float32(ROPE_BASE), np.arange(HD // 2, dtype=np.float32) * np.float32(2.0 / HD)
    freqs = np.power(base, -power).astype(np.float32)
    angles = np.arange(tokens, dtype=np.float32)[:, None] * freqs[None, :]
    cosine, sine = np.cos(angles), np.sin(angles)
    cosine = jnp.asarray(np.concatenate([cosine, cosine], axis=1))
    sine = jnp.asarray(np.concatenate([-sine, sine], axis=1))
    bias = jnp.concatenate([bias_key, bias_value, bias_query])[None, :]

    rows = w_query.shape[0]
    heads_cols = w_query.shape[1]
    slabs = 1 + heads_cols // PIECE
    pieces = len(cut(slabs))
    any_spec = pl.BlockSpec(memory_space=pl.ANY)
    vmem = pl.BlockSpec(memory_space=pltpu.VMEM)
    smem = pl.BlockSpec(memory_space=pltpu.SMEM)
    dma = pltpu.SemaphoreType.DMA
    keys, vals, got, got_label = pl.pallas_call(
        functools.partial(fused_kernel, n, tp, pair),
        out_shape=[
            jax.ShapeDtypeStruct((tokens, HD), jnp.bfloat16),
            jax.ShapeDtypeStruct((tokens, HD), jnp.bfloat16),
            jax.ShapeDtypeStruct((slabs - 1, n, pair, block, PIECE), jnp.bfloat16),
            jax.ShapeDtypeStruct((n, 8, 128), jnp.int32),
        ],
        in_specs=[smem, any_spec, any_spec, any_spec, any_spec, vmem, vmem, vmem, vmem, any_spec],
        out_specs=[vmem, vmem, any_spec, any_spec],
        scratch_shapes=[
            pltpu.VMEM((tp, tokens, part), jnp.bfloat16),
            pltpu.VMEM((tokens, tp * part), jnp.bfloat16),
            pltpu.VMEM((slabs, n * rows, PIECE), jnp.bfloat16),
            pltpu.VMEM((tokens, PIECE), jnp.bfloat16),
            pltpu.VMEM((owned, block, PIECE), jnp.bfloat16),
            pltpu.VMEM((slabs - 1, n, pair, block, PIECE), jnp.bfloat16),
            dma((pieces + 2,)),
            dma((3,)),
            dma((3,)),
            dma((pieces, 2, n - 1)),
            dma((pieces, 2, n - 1)),
            dma((pieces, 2, n - 1)),
            dma((pieces, 2, n - 1)),
            dma((pieces - 1, n)),
            dma((pieces - 1, n)),
            dma((n,)),
            dma((n,)),
        ],
        compiler_params=pltpu.CompilerParams(
            collective_id=0, has_side_effects=True, vmem_limit_bytes=56 * 1024 * 1024
        ),
    )(
        source,
        hidden.reshape(tokens, part),
        w_query,
        w_key,
        w_value,
        norm_gain[None, :],
        bias,
        cosine,
        sine,
        label,
    )

    perm = cache_slot[0]
    inverse = jnp.sum(jnp.where(perm[None, :] == slots[:, None], slots[None, :], 0), axis=1)
    zero_half = jnp.zeros((), jnp.bfloat16)
    live_blocks = (inverse < prefix_blocks[0])[:, None, None]
    keys = keys.reshape(owned, block, -1)
    vals = vals.reshape(owned, block, -1)
    key_cache = jnp.where(live_blocks, jnp.take(keys, inverse, axis=0), zero_half)
    value_cache = jnp.where(live_blocks, jnp.take(vals, inverse, axis=0), zero_half)
    labels = got_label[:, 0, :pair].reshape(-1)
    wanted = labels[None, :] == jnp.arange(BAL, dtype=jnp.int32)[:, None]
    chosen = jnp.sum(jnp.where(wanted, items[None, :], 0), axis=1)
    got = got.reshape(slabs - 1, n * pair, block, PIECE)
    attn_out = jnp.take(got, chosen, axis=1)
    attn_out = jnp.moveaxis(attn_out, 0, 2).reshape(BAL, block, heads_cols)
    return (attn_out, key_cache, value_cache)


def solution(mesh):
    small = mesh.shape["inst"] == 4 and mesh.shape["tp"] == 4 and mesh.shape["groups"] == 2
    in_specs = (
        P(("groups", "inst"), None, "tp"),
        P(),
        P("inst", "tp"),
        P("inst", "tp"),
        P("inst", "tp"),
        P("tp"),
        P("tp"),
        P("tp"),
        P(("groups", "inst")),
        P(("groups", "inst"), None),
        P(("groups", "inst"), None),
    )
    out_specs = (
        P(("groups", "inst"), None, "tp"),
        P(("groups", "inst"), None, "tp"),
        P(("groups", "inst"), None, "tp"),
    )
    body = fused if small else shards
    return jax.shard_map(body, mesh=mesh, in_specs=in_specs, out_specs=out_specs, check_vma=False)
```

```python
import functools
import math

import jax
import jax.numpy as jnp
import numpy as np
from jax import lax
from jax.experimental import pallas as pl
from jax.experimental.pallas import tpu as pltpu
from jax.sharding import PartitionSpec as P

HD = 128
BAL = 12


ROPE_BASE = 1000000.0
NORM_EPS = 1e-06


def rotate(values, positions):
    width = values.shape[-1]
    half = width // 2
    freqs = ROPE_BASE ** (-(jnp.arange(half, dtype=jnp.float32) * 2.0 / width))
    angles = positions.astype(jnp.float32)[:, None] * freqs[None, :]
    cosine = jnp.cos(angles)[:, None, :]
    sine = jnp.sin(angles)[:, None, :]
    first = values[..., :half]
    second = values[..., half:]
    return jnp.concatenate(
        [first * cosine - second * sine, second * cosine + first * sine], axis=-1
    )


def project(whole, positions, norm_gain, w_query, w_key, w_value, bias_query, bias_key, bias_value):
    values = whole.astype(jnp.float32)
    inverse_rms = lax.rsqrt(jnp.mean(values * values, axis=-1, keepdims=True) + NORM_EPS)
    normed = (values * inverse_rms * norm_gain).astype(jnp.bfloat16)
    total_rows = normed.shape[0]
    query_sum = jnp.dot(
        normed,
        lax.all_gather(w_query, "inst", axis=0, tiled=True),
        preferred_element_type=jnp.float32,
    )
    key_sum = jnp.dot(
        normed,
        lax.all_gather(w_key, "inst", axis=0, tiled=True),
        preferred_element_type=jnp.float32,
    )
    value_sum = jnp.dot(
        normed,
        lax.all_gather(w_value, "inst", axis=0, tiled=True),
        preferred_element_type=jnp.float32,
    )
    query = query_sum
    keys = key_sum
    vals = value_sum
    query = rotate((query + bias_query).reshape(total_rows, -1, HD), positions)
    query = query.reshape(total_rows, -1).astype(jnp.bfloat16)
    keys = rotate((keys + bias_key).reshape(total_rows, -1, HD), positions)
    keys = keys.reshape(total_rows, -1).astype(jnp.bfloat16)
    vals = (vals + bias_value).astype(jnp.bfloat16)
    return (query, keys, vals)


def pick_slots(labels_place, labels_live, count):
    items = jnp.arange(labels_place.shape[0], dtype=jnp.int32)
    wanted = (labels_place[None, :] == jnp.arange(count, dtype=jnp.int32)[:, None]) & (
        labels_live[None, :] == 1
    )
    return jnp.sum(jnp.where(wanted, items[None, :], 0), axis=1)


def shards(
    hidden,
    norm_gain,
    w_query,
    w_key,
    w_value,
    bias_query,
    bias_key,
    bias_value,
    prefix_blocks,
    block_target,
    cache_slot,
):
    owned, width_block, part_width = hidden.shape
    peers = lax.axis_size("inst")
    pair = -(-owned // peers)
    total_rows = owned * width_block
    slots = jnp.arange(owned, dtype=jnp.int32)
    live = slots < prefix_blocks[0]
    target = block_target[0]
    dest = jnp.where(live, target // BAL, -1)
    place = jnp.where(live, target % BAL, 0)
    earlier = (dest[:, None] == dest[None, :]) & live[None, :] & (slots[None, :] < slots[:, None])
    rank = jnp.sum(earlier.astype(jnp.int32), axis=1)
    item_of_slot = jnp.where(live, dest * pair + rank, -1)
    items = jnp.arange(peers * pair, dtype=jnp.int32)
    matched = item_of_slot[None, :] == items[:, None]
    present = jnp.any(matched, axis=1)
    source = jnp.sum(jnp.where(matched, slots[None, :], 0), axis=1)
    own_positions = jnp.arange(total_rows, dtype=jnp.int32)
    zero_half = jnp.zeros((), jnp.bfloat16)
    whole = lax.all_gather(hidden.reshape(total_rows, part_width), "tp", axis=1, tiled=True)
    query, keys, vals = project(
        whole, own_positions, norm_gain, w_query, w_key, w_value, bias_query, bias_key, bias_value
    )
    kv_here = keys.shape[1] // HD
    group = query.shape[1] // (HD * kv_here)
    query_heads = query.reshape(total_rows, kv_here, group, HD)
    key_heads = keys.reshape(total_rows, kv_here, HD)
    value_heads = vals.reshape(total_rows, kv_here, HD)
    causal = own_positions[:, None] >= own_positions[None, :]
    scale_factor = 1.0 / math.sqrt(HD)

    def head(query_group):
        scores = (
            jnp.einsum("rkd,skd->krs", query_group, key_heads, preferred_element_type=jnp.float32)
            * scale_factor
        )
        scores = jnp.where(causal[None], scores, -jnp.inf)
        largest = jnp.max(scores, axis=-1, keepdims=True)
        expo = jnp.exp(scores - largest)
        probs = (expo / jnp.sum(expo, axis=-1, keepdims=True)).astype(jnp.bfloat16)
        mixed = jnp.einsum("krs,skd->rkd", probs, value_heads, preferred_element_type=jnp.float32)
        return mixed.astype(jnp.bfloat16)

    heads_out = lax.map(head, jnp.moveaxis(query_heads, 2, 0))
    attention = jnp.transpose(heads_out, (1, 2, 0, 3)).reshape(owned, width_block, -1)
    perm = cache_slot[0]
    inverse = jnp.sum(jnp.where(perm[None, :] == slots[:, None], slots[None, :], 0), axis=1)
    live_blocks = live[:, None, None]
    key_blocks = jnp.where(live_blocks, keys.reshape(owned, width_block, -1), zero_half)
    value_blocks = jnp.where(live_blocks, vals.reshape(owned, width_block, -1), zero_half)
    key_cache = jnp.take(key_blocks, inverse, axis=0)
    value_cache = jnp.take(value_blocks, inverse, axis=0)
    send_out = jnp.where(present[:, None, None], jnp.take(attention, source, axis=0), zero_half)
    send_out = send_out.reshape(peers, pair, width_block, -1)
    out_labels = jnp.stack([jnp.take(place, source), present.astype(jnp.int32)], axis=-1).reshape(
        peers, pair, 2
    )
    got_out, got_out_labels = (
        lax.all_to_all(send_out, "inst", split_axis=0, concat_axis=0, tiled=True),
        lax.all_to_all(out_labels, "inst", split_axis=0, concat_axis=0, tiled=True),
    )
    got_out = got_out.reshape(peers * pair, width_block, -1)
    got_out_labels = got_out_labels.reshape(peers * pair, 2)
    chosen_out = pick_slots(got_out_labels[:, 0], got_out_labels[:, 1], BAL)
    attn_out = jnp.take(got_out, chosen_out, axis=0)
    return (attn_out, key_cache, value_cache)


TILE = 256
PIECE = 256
MESH = pl.DeviceIdType.MESH


def cut(slabs):
    whole = [(k, 0, PIECE) for k in range(slabs - 1)]
    return whole + [(slabs - 1, 0, HD), (slabs - 1, HD, HD)]


def fused_kernel(
    n,
    tp,
    pair,
    source_ref,
    cache_ref,
    hid_ref,
    wq_ref,
    wk_ref,
    wv_ref,
    gain_ref,
    bias_ref,
    cos_ref,
    sin_ref,
    lab_ref,
    key_out,
    val_out,
    got_ref,
    lab_out,
    key_ref,
    val_ref,
    kv_blocks,
    hbuf,
    normed,
    wfull,
    qbuf,
    atb,
    sendbuf,
    loc_sem,
    h_send,
    h_recv,
    z_send,
    z_recv,
    y_send,
    y_recv,
    d_send,
    d_recv,
    l_send,
    l_recv,
):
    g = lax.axis_index("groups")
    i = lax.axis_index("inst")
    t = lax.axis_index("tp")
    x, core = t // 2, t % 2
    t_core = 2 * x + (1 - core)
    t_far = 2 * (1 - x) + core
    t_diag = 2 * (1 - x) + (1 - core)
    tokens, part = hid_ref.shape
    rows = wq_ref.shape[0]
    half = rows // 2
    parts = cut(wfull.shape[0])
    pieces = len(parts)
    peers_inst = [b for b in range(n)]

    local = [pltpu.make_async_copy(hid_ref, hbuf.at[t], loc_sem.at[0])]
    own = pl.ds(pl.multiple_of(i * rows, rows), rows)
    local.append(pltpu.make_async_copy(wk_ref, wfull.at[0, own, pl.ds(0, HD)], loc_sem.at[1]))
    local.append(pltpu.make_async_copy(wv_ref, wfull.at[0, own, pl.ds(HD, HD)], loc_sem.at[2]))
    for c in range(1, pieces):
        local.append(
            pltpu.make_async_copy(
                wq_ref.at[:, pl.ds((parts[c][0] - 1) * PIECE + parts[c][1], parts[c][2])],
                wfull.at[parts[c][0], own, pl.ds(parts[c][1], parts[c][2])],
                loc_sem.at[c + 2],
            )
        )
    for copy in local:
        copy.start()

    barrier = pltpu.get_barrier_semaphore()
    for b in peers_inst:

        @pl.when(i != b)
        def _():
            pl.semaphore_signal(barrier, inc=1, device_id=(g, b, t), device_id_type=MESH)

    for other in ((1 - g, i, t), (g, i, t_core), (g, i, t_far)):
        pl.semaphore_signal(barrier, inc=1, device_id=other, device_id_type=MESH)
    pl.semaphore_wait(barrier, n - 1 + 3)

    pending = []

    def start(cond, make):
        pending.append((cond, make))
        if cond is None:
            make().start()
        else:

            @pl.when(cond)
            def _():
                make().start()

    def arrive(cond, make):
        @pl.when(cond)
        def _():
            make().wait_recv()

    def piece(c, j, h):
        slab, off, width = parts[c]
        here = pl.ds(pl.multiple_of(j * rows + h * half, half), half)
        return wfull.at[slab, here, pl.ds(off, width)]

    def z_copy(c, d, s, j):
        to = i + 1 if d == 0 else i - 1
        return pltpu.make_async_remote_copy(
            src_ref=piece(c, j, g),
            dst_ref=piece(c, j, g),
            send_sem=z_send.at[c, d, s],
            recv_sem=z_recv.at[c, d, s],
            device_id=(g, to, t),
            device_id_type=MESH,
        )

    def y_copy(c, d, s, j, h):
        return pltpu.make_async_remote_copy(
            src_ref=piece(c, j, h),
            dst_ref=piece(c, j, h),
            send_sem=y_send.at[c, d, s],
            recv_sem=y_recv.at[c, d, s],
            device_id=(1 - g, i, t),
            device_id_type=MESH,
        )

    def hid_copy(k, slot, to):
        return pltpu.make_async_remote_copy(
            src_ref=hbuf.at[slot],
            dst_ref=hbuf.at[slot],
            send_sem=h_send.at[k],
            recv_sem=h_recv.at[k],
            device_id=(g, i, to),
            device_id_type=MESH,
        )

    def send_z(c, s):
        start((i - s >= 0) & (i < n - 1), functools.partial(z_copy, c, 0, s, i - s))
        start((i + s <= n - 1) & (i > 0), functools.partial(z_copy, c, 1, s, i + s))

    def comm(c, s):
        for d in range(2):
            j = i - 1 - s if d == 0 else i + 1 + s
            have = j >= 0 if d == 0 else j <= n - 1
            arrive(have, functools.partial(z_copy, c, d, s, j))
            if s + 1 < n - 1:
                onward = have & ((i < n - 1) if d == 0 else (i > 0))
                start(onward, functools.partial(z_copy, c, d, s + 1, j))
            start(have, functools.partial(y_copy, c, d, s, j, g))

    def settle(c):
        for s in range(n - 1):
            for d in range(2):
                j = i - 1 - s if d == 0 else i + 1 + s
                have = j >= 0 if d == 0 else j <= n - 1
                arrive(have, functools.partial(y_copy, c, d, s, j, 1 - g))

    def norm():
        @pl.loop(0, tokens // 32)
        def _(r):
            here = pl.ds(pl.multiple_of(r * 32, 32), 32)
            total = jnp.zeros((32, 1), jnp.float32)
            for p in range(tp):
                v = hbuf[p, here, :].astype(jnp.float32)
                total = total + jnp.sum(v * v, axis=-1, keepdims=True)
            inverse = lax.rsqrt(total / (tp * part) + NORM_EPS)
            for p in range(tp):
                cols = pl.ds(p * part, part)
                v = hbuf[p, here, :].astype(jnp.float32)
                normed[here, cols] = (v * inverse * gain_ref[:, cols]).astype(jnp.bfloat16)

    def turn(v, here):
        return v * cos_ref[here, :] + pltpu.roll(v, HD // 2, 1) * sin_ref[here, :]

    def product(c):
        settle(c)
        slab, off, width = parts[c]

        @pl.loop(0, tokens // TILE)
        def _(r):
            here = pl.ds(pl.multiple_of(r * TILE, TILE), TILE)
            acc = jnp.dot(
                normed[here, :],
                wfull[slab, :, pl.ds(off, width)],
                preferred_element_type=jnp.float32,
            )
            acc = acc + bias_ref[:, pl.ds(slab * PIECE + off, width)]
            if c == 0:
                k_new = turn(acc[:, :HD], here).astype(jnp.bfloat16)
                v_new = acc[:, HD:].astype(jnp.bfloat16)
                key_ref[here, :] = k_new
                val_ref[here, :] = v_new
                block = kv_blocks.shape[2]
                count = TILE // block
                there = pl.ds(r * count, count)
                kv_blocks[0, there] = k_new.reshape(count, block, HD)
                kv_blocks[1, there] = v_new.reshape(count, block, HD)
            else:
                for head in range(width // HD):
                    cols = slice(head * HD, (head + 1) * HD)
                    qbuf[here, cols] = turn(acc[:, cols], here).astype(jnp.bfloat16)

    def attend(c):
        scale = 1.0 / math.sqrt(HD)
        rr = lax.broadcasted_iota(jnp.int32, (TILE, TILE), 0)
        cc = lax.broadcasted_iota(jnp.int32, (TILE, TILE), 1)
        block = atb.shape[1]
        for r in range(tokens // TILE):
            for head in range(parts[c][2] // HD):
                q = qbuf[pl.ds(r * TILE, TILE), pl.ds(head * HD, HD)]
                width = (r + 1) * TILE
                sc = (
                    lax.dot_general(
                        q,
                        key_ref[pl.ds(0, width), :],
                        (((1,), (1,)), ((), ())),
                        preferred_element_type=jnp.float32,
                    )
                    * scale
                )
                last = jnp.where(rr >= cc, sc[:, width - TILE :], -jnp.inf)
                sc = last if r == 0 else jnp.concatenate([sc[:, : width - TILE], last], axis=1)
                expo = jnp.exp(sc - jnp.max(sc, axis=-1, keepdims=True))
                probs = (expo / jnp.sum(expo, axis=-1, keepdims=True)).astype(jnp.bfloat16)
                mixed = jnp.dot(
                    probs, val_ref[pl.ds(0, width), :], preferred_element_type=jnp.float32
                ).astype(jnp.bfloat16)
                atb[pl.ds(r * (TILE // block), TILE // block), :, pl.ds(head * HD, HD)] = (
                    mixed.reshape(TILE // block, block, HD)
                )

    def packed(q, b):
        slab, off, width = parts[q + 1]
        return sendbuf.at[slab - 1, b, :, :, pl.ds(off, width)]

    def landed(q, b):
        slab, off, width = parts[q + 1]
        return got_ref.at[slab - 1, b, :, :, pl.ds(off, width)]

    def d_copy(q, b):
        return pltpu.make_async_remote_copy(
            src_ref=packed(q, b),
            dst_ref=landed(q, i),
            send_sem=d_send.at[q, b],
            recv_sem=d_recv.at[q, i],
            device_id=(g, b, t),
            device_id_type=MESH,
        )

    def d_wait(q, b):
        return pltpu.make_async_remote_copy(
            src_ref=packed(q, b),
            dst_ref=landed(q, b),
            send_sem=d_send.at[q, b],
            recv_sem=d_recv.at[q, b],
            device_id=(g, b, t),
            device_id_type=MESH,
        )

    def stay(q, b):
        return pltpu.make_async_copy(packed(q, b), landed(q, b), d_send.at[q, b])

    def l_copy(b):
        return pltpu.make_async_remote_copy(
            src_ref=lab_ref.at[b],
            dst_ref=lab_out.at[i],
            send_sem=l_send.at[b],
            recv_sem=l_recv.at[i],
            device_id=(g, b, t),
            device_id_type=MESH,
        )

    def l_wait(b):
        return pltpu.make_async_remote_copy(
            src_ref=lab_ref.at[b],
            dst_ref=lab_out.at[b],
            send_sem=l_send.at[b],
            recv_sem=l_recv.at[b],
            device_id=(g, b, t),
            device_id_type=MESH,
        )

    def l_stay(b):
        return pltpu.make_async_copy(lab_ref.at[b], lab_out.at[b], l_send.at[b])

    def dispatch(q):
        slab, off, width = parts[q + 1]
        for b in peers_inst:
            for k in range(pair):
                sendbuf[slab - 1, b, k, :, pl.ds(off, width)] = atb[
                    source_ref[b * pair + k], :, pl.ds(0, width)
                ]
            start(i != b, functools.partial(d_copy, q, b))

            @pl.when(i == b)
            def _():
                stay(q, b).start()

    local[0].wait()
    start(None, functools.partial(hid_copy, 0, t, t_far))
    start(None, functools.partial(hid_copy, 1, t, t_core))
    for copy in local[1:]:
        copy.wait()
    send_z(0, 0)
    send_z(1, 0)
    for b in peers_inst:
        start(i != b, functools.partial(l_copy, b))

        @pl.when(i == b)
        def _():
            l_stay(b).start()

    send_z(2, 0)
    last = n - 1

    def comms(c, first=0):
        for s in range(first, last):
            comm(c, s)

    comms(0)
    send_z(3, 0)
    comms(1)
    hid_copy(0, t_far, t_far).wait_recv()
    start(None, functools.partial(hid_copy, 2, t_far, t_core))
    for c in range(4, pieces):
        send_z(c, 0)
    hid_copy(1, t_core, t_core).wait_recv()
    hid_copy(2, t_diag, t_core).wait_recv()
    norm()
    comm(2, 0)
    product(0)
    owned = key_out.shape[0]
    for which, out in enumerate((key_out, val_out)):
        kv_blocks[which, owned] = jnp.zeros(kv_blocks.shape[2:], jnp.bfloat16)
        for k in range(owned):
            out[k] = kv_blocks[which, cache_ref[k]]
    comms(2, 1)
    for c in range(1, pieces):
        ahead = c + 2
        if ahead < pieces:
            comm(ahead, 0)
        product(c)
        if ahead < pieces:
            comm(ahead, 1)
        attend(c)
        dispatch(c - 1)
        if ahead < pieces:
            comms(ahead, 2)

    for b in peers_inst:

        @pl.when(i != b)
        def _():
            l_wait(b).wait_recv()
            for q in range(pieces - 1):
                d_wait(q, b).wait_recv()

        @pl.when(i == b)
        def _():
            l_stay(b).wait()
            for q in range(pieces - 1):
                stay(q, b).wait()

    for cond, make in pending:
        if cond is None:
            make().wait_send()
        else:

            @pl.when(cond)
            def _():
                make().wait_send()


def fused(
    hidden,
    norm_gain,
    w_query,
    w_key,
    w_value,
    bias_query,
    bias_key,
    bias_value,
    prefix_blocks,
    block_target,
    cache_slot,
):
    owned, block, part = hidden.shape
    n = lax.axis_size("inst")
    tp = lax.axis_size("tp")
    pair = -(-owned // n)
    tokens = owned * block
    slots = jnp.arange(owned, dtype=jnp.int32)
    live = slots < prefix_blocks[0]
    target = block_target[0]
    dest = jnp.where(live, target // BAL, -1)
    place = jnp.where(live, target % BAL, 0)
    earlier = (dest[:, None] == dest[None, :]) & live[None, :] & (slots[None, :] < slots[:, None])
    rank = jnp.sum(earlier.astype(jnp.int32), axis=1)
    item_of_slot = jnp.where(live, dest * pair + rank, -1)
    items = jnp.arange(n * pair, dtype=jnp.int32)
    matched = item_of_slot[None, :] == items[:, None]
    present = jnp.any(matched, axis=1)
    source = jnp.sum(jnp.where(matched, slots[None, :], 0), axis=1)
    item_place = jnp.sum(jnp.where(matched, place[None, :], 0), axis=1)
    label = jnp.where(present, item_place, -1).reshape(n, 1, pair)
    label = jnp.pad(label, ((0, 0), (0, 7), (0, 128 - pair)), constant_values=-1)

    base, power = np.float32(ROPE_BASE), np.arange(HD // 2, dtype=np.float32) * np.float32(2.0 / HD)
    freqs = np.power(base, -power).astype(np.float32)
    angles = np.arange(tokens, dtype=np.float32)[:, None] * freqs[None, :]
    cosine, sine = np.cos(angles), np.sin(angles)
    cosine = jnp.asarray(np.concatenate([cosine, cosine], axis=1))
    sine = jnp.asarray(np.concatenate([-sine, sine], axis=1))
    bias = jnp.concatenate([bias_key, bias_value, bias_query])[None, :]

    perm = cache_slot[0]
    kept = (perm[None, :] == slots[:, None]) & live[None, :]
    cache_block = owned + jnp.sum(jnp.where(kept, slots[None, :] - owned, 0), axis=1)
    rows = w_query.shape[0]
    heads_cols = w_query.shape[1]
    slabs = 1 + heads_cols // PIECE
    pieces = len(cut(slabs))
    any_spec = pl.BlockSpec(memory_space=pl.ANY)
    vmem = pl.BlockSpec(memory_space=pltpu.VMEM)
    smem = pl.BlockSpec(memory_space=pltpu.SMEM)
    dma = pltpu.SemaphoreType.DMA
    key_cache, value_cache, got, got_label = pl.pallas_call(
        functools.partial(fused_kernel, n, tp, pair),
        out_shape=[
            jax.ShapeDtypeStruct((owned, block, HD), jnp.bfloat16),
            jax.ShapeDtypeStruct((owned, block, HD), jnp.bfloat16),
            jax.ShapeDtypeStruct((slabs - 1, n, pair, block, PIECE), jnp.bfloat16),
            jax.ShapeDtypeStruct((n, 8, 128), jnp.int32),
        ],
        in_specs=[smem, smem, any_spec, any_spec, any_spec, any_spec, vmem, vmem, vmem, vmem, any_spec],
        out_specs=[vmem, vmem, any_spec, any_spec],
        scratch_shapes=[
            pltpu.VMEM((tokens, HD), jnp.bfloat16),
            pltpu.VMEM((tokens, HD), jnp.bfloat16),
            pltpu.VMEM((2, owned + 1, block, HD), jnp.bfloat16),
            pltpu.VMEM((tp, tokens, part), jnp.bfloat16),
            pltpu.VMEM((tokens, tp * part), jnp.bfloat16),
            pltpu.VMEM((slabs, n * rows, PIECE), jnp.bfloat16),
            pltpu.VMEM((tokens, PIECE), jnp.bfloat16),
            pltpu.VMEM((owned, block, PIECE), jnp.bfloat16),
            pltpu.VMEM((slabs - 1, n, pair, block, PIECE), jnp.bfloat16),
            dma((pieces + 2,)),
            dma((3,)),
            dma((3,)),
            dma((pieces, 2, n - 1)),
            dma((pieces, 2, n - 1)),
            dma((pieces, 2, n - 1)),
            dma((pieces, 2, n - 1)),
            dma((pieces - 1, n)),
            dma((pieces - 1, n)),
            dma((n,)),
            dma((n,)),
        ],
        compiler_params=pltpu.CompilerParams(
            collective_id=0, has_side_effects=True, vmem_limit_bytes=56 * 1024 * 1024
        ),
    )(
        source,
        cache_block,
        hidden.reshape(tokens, part),
        w_query,
        w_key,
        w_value,
        norm_gain[None, :],
        bias,
        cosine,
        sine,
        label,
    )

    labels = got_label[:, 0, :pair].reshape(-1)
    wanted = labels[None, :] == jnp.arange(BAL, dtype=jnp.int32)[:, None]
    chosen = jnp.sum(jnp.where(wanted, items[None, :], 0), axis=1)
    got = got.reshape(slabs - 1, n * pair, block, PIECE)
    attn_out = jnp.take(got, chosen, axis=1)
    attn_out = jnp.moveaxis(attn_out, 0, 2).reshape(BAL, block, heads_cols)
    return (attn_out, key_cache, value_cache)


def solution(mesh):
    small = mesh.shape["inst"] == 4 and mesh.shape["tp"] == 4 and mesh.shape["groups"] == 2
    in_specs = (
        P(("groups", "inst"), None, "tp"),
        P(),
        P("inst", "tp"),
        P("inst", "tp"),
        P("inst", "tp"),
        P("tp"),
        P("tp"),
        P("tp"),
        P(("groups", "inst")),
        P(("groups", "inst"), None),
        P(("groups", "inst"), None),
    )
    out_specs = (
        P(("groups", "inst"), None, "tp"),
        P(("groups", "inst"), None, "tp"),
        P(("groups", "inst"), None, "tp"),
    )
    body = fused if small else shards
    return jax.shard_map(body, mesh=mesh, in_specs=in_specs, out_specs=out_specs, check_vma=False)
```
